128 devices in a mesh: gx: 16 (over y, x), gy: 8 (over z, core).
Axes of the slice: x: 4, y: 4, z: 4, core: 2. Of those that a mesh axis runs over, the one named last changes fastest.
Arguments:
- melt_field: float32 [4096, 256, 256], P('gx', 'gy'), may hold values from -90 to 90
- start_time: float32 [256, 32], replicated, may hold values from -6 to 6
- start_x: float32 [4096, 256], P('gx'), may hold values from -6 to 6
Outputs:
- time_basis: float32 [256, 32], replicated
- x_basis: float32 [4096, 256], P('gx')
- core: float32 [256, 8192], P('gx', 'gy')
The draws below stay inside these ranges and needn't reach their ends.
All inputs are finite; a program needn't handle non-finite values.
Results may differ from the reference program's by a relative error of at most 0.0003.
Values sent between devices are 32-bit elements; how exact they have to be, the bound alone decides.
No kernel may reach another device: no remote copies, remote signals or barrier semaphores. Data moves between devices by JAX's collectives and lax.ppermute only.
A program may use at most 128 MiB of HBM per device.

```python
import math
import jax
import jax.numpy as jnp
from jax import lax

TLEN = 256
R_T = 32
R_X = 256
ITERS_T = 8
SWEEPS_X = 3
NX = 4096
NY = 256


def draw_melt_field(key, part):
    key = jax.random.fold_in(key, 11)
    keys = jax.random.split(key, 4)
    scale_x = jnp.exp(jax.random.uniform(keys[0], (NX, 1, 1), jnp.float32, 0.0, math.log(3.0)))
    scale_y = jnp.exp(jax.random.uniform(keys[1], (1, NY, 1), jnp.float32, 0.0, math.log(3.0)))
    scale_t = jnp.exp(jax.random.uniform(keys[2], (1, 1, TLEN), jnp.float32, math.log(0.5), math.log(2.0)))
    values = jnp.clip(jax.random.normal(keys[3], (NX, NY, TLEN), jnp.float32), -5.0, 5.0)
    return (values * scale_x * scale_y * scale_t).astype(jnp.float32)


def levels(rng, dims, shards, least, high):
    loudness = 1.0
    for dim, blocks in shards:
        steps = jax.random.uniform(jax.random.fold_in(jax.random.fold_in(rng, 6), dim), (blocks,), jnp.float32, least / len(shards), high / len(shards))
        loudness = loudness * jnp.repeat(jnp.exp(steps), dims[dim] // blocks).reshape((-1,) + (1,) * (len(dims) - 1 - dim))
    return loudness


def bell_draw(own_key, shape, spread, limit, pieces=(), kind=jnp.bfloat16):
    array = spread * jax.random.normal(own_key, shape, jnp.float32)
    if pieces:
        array = array * levels(own_key, shape, pieces, -0.22, 0.18)
    return jnp.clip(array, -limit, limit).astype(kind)


def setup_inputs(seed: int = 0) -> dict:
    key_list = jax.random.split(jax.random.key(seed), 4)
    return {
        "melt_field": draw_melt_field(jax.random.fold_in(key_list[3], 71), 0),
        "start_time": bell_draw(key_list[1], (TLEN, R_T), 1.0, 6.0, (), jnp.float32),
        "start_x": bell_draw(key_list[2], (NX, R_X), 1.0, 6.0, ((0, 16),), jnp.float32),
    }


def precise_dot(left, right):
    return jnp.dot(left.astype(jnp.float32), right.astype(jnp.float32), precision=lax.Precision.HIGHEST, preferred_element_type=jnp.float32)

def inner_dot(left, right):
    return lax.dot_general(left.astype(jnp.float32), right.astype(jnp.float32), (((0,), (0,)), ((), ())), precision=lax.Precision.HIGHEST, preferred_element_type=jnp.float32)

def orthonormal(applied, cross_prod):
    factor = jnp.linalg.cholesky(cross_prod)
    return lax.linalg.triangular_solve(factor, applied, left_side=False, lower=True, transpose_a=True)

def subspace(gram_matrix, begin_block, repeats):
    current = begin_block
    for repeat in range(repeats):
        applied = precise_dot(gram_matrix, current)
        current = orthonormal(applied, inner_dot(applied, applied))
    return current

def reference(melt_field, start_time, start_x):
    flattened = melt_field.reshape(NX * NY, TLEN)
    gram_time = inner_dot(flattened, flattened)
    time_basis = subspace(gram_time, start_time, ITERS_T)
    shrunk = precise_dot(flattened, time_basis).reshape(NX, NY * R_T)
    gram_x = lax.dot_general(shrunk.astype(jnp.float32), shrunk.astype(jnp.float32), (((1,), (1,)), ((), ())), precision=lax.Precision.HIGHEST, preferred_element_type=jnp.float32)
    x_basis = subspace(gram_x, start_x, SWEEPS_X)
    core = inner_dot(x_basis, shrunk)
    return (time_basis, x_basis, core)
```

```python
import functools

import jax
import jax.numpy as jnp
from jax import lax
from jax.experimental import pallas as pl
from jax.experimental.pallas import tpu as pltpu
from jax.sharding import PartitionSpec as P

ITERS_T = 8
SWEEPS_X = 3
F32 = jnp.float32
BF16 = jnp.bfloat16
HI = lax.Precision.HIGHEST


def split3(x):
    h = x.astype(BF16)
    rest = x - h.astype(F32)
    m = rest.astype(BF16)
    l = (rest - m.astype(F32)).astype(BF16)
    return h, m, l


def split2(x):
    h = x.astype(BF16)
    return h, (x - h.astype(F32)).astype(BF16)


def dot(a, b, ca=1, cb=0):
    return lax.dot_general(a, b, (((ca,), (cb,)), ((), ())), preferred_element_type=F32)


def packed_rhs(b):
    h, m, l = b
    return jnp.concatenate([h, m, h, m, l, h], axis=0)


def packed_lhs(a, axis):
    h, m, l = a
    return jnp.concatenate([h, h, m, m, h, l], axis=axis)


def inverse_factor(gram):
    n = gram.shape[0]
    tiles = n // 8
    left = [gram[8 * t : 8 * t + 8] for t in range(tiles)]
    row_id = lax.broadcasted_iota(jnp.int32, (8, n), 0)
    col_id = lax.broadcasted_iota(jnp.int32, (8, n), 1)
    right = [jnp.where(col_id == row_id + 8 * t, 1.0, 0.0).astype(F32) for t in range(tiles)]
    out = []
    for b in range(tiles):
        cols = {
            t: [jnp.broadcast_to(left[t][:, 8 * b + m : 8 * b + m + 1], (8, n)) for m in range(8)]
            for t in range(b, tiles)
        }
        rows_l, rows_r = left[b], right[b]
        steps = []
        scale = jnp.ones((8, n), F32)
        for m in range(8):
            pivot = jnp.broadcast_to(cols[b][m][m : m + 1], (8, n))
            inv = 1.0 / pivot
            scale = jnp.where(row_id == m, lax.rsqrt(pivot), scale)
            factor = {t: cols[t][m] * inv for t in range(b, tiles)}
            factor[b] = jnp.where(row_id > m, factor[b], 0.0)
            for n2 in range(m + 1, 8):
                value = jnp.broadcast_to(cols[b][n2][m : m + 1], (8, n))
                for t in range(b, tiles):
                    cols[t][n2] = cols[t][n2] - factor[t] * value
            row_l = jnp.broadcast_to(rows_l[m : m + 1], (8, n))
            row_r = jnp.broadcast_to(rows_r[m : m + 1], (8, n))
            rows_l = rows_l - factor[b] * row_l
            rows_r = rows_r - factor[b] * row_r
            steps.append((factor, row_l, row_r))
        for t in range(b + 1, tiles):
            for factor, row_l, row_r in steps:
                left[t] = left[t] - factor[t] * row_l
                right[t] = right[t] - factor[t] * row_r
        out.append(rows_r * scale)
    return jnp.concatenate(out, axis=0)


BLK = 32


def chol_kernel(c_ref, out_ref, work):
    n = c_ref.shape[0]
    col_id = lax.broadcasted_iota(jnp.int32, (BLK, n), 1)
    row_id = lax.broadcasted_iota(jnp.int32, (BLK, n), 0)
    work[...] = c_ref[...]
    diag = work[0:BLK, 0:BLK]
    for k in range(n // BLK):
        lo, hi = k * BLK, (k + 1) * BLK
        inv = inverse_factor(diag)
        in_blk = (col_id >= lo) & (col_id < hi)
        row = jnp.where(in_blk, jnp.where(col_id - lo == row_id, 1.0, 0.0), work[lo:hi, :])
        r = dot(packed_lhs(split3(inv), 1), packed_rhs(split3(row)))
        out_ref[lo:hi, :] = jnp.where(col_id < hi, r, 0.0)
        if hi < n:
            parts = split3(r)
            xt, w = packed_lhs(parts, 0), packed_rhs(parts)
            small = dot(xt[:, hi : hi + BLK], w[:, hi : hi + BLK], 0, 0)
            diag = work[hi : hi + BLK, hi : hi + BLK] - small
            base = hi // 128 * 128
            upd = dot(xt[:, base:], w, 0, 0)
            cid = lax.broadcasted_iota(jnp.int32, (n - hi, n), 1)
            old = jnp.where((cid >= lo) & (cid < hi), 0.0, work[hi:, :])
            work[hi:, :] = old - upd[hi - base :, :]


def chol_inverse(c):
    n = c.shape[0]
    return pl.pallas_call(
        chol_kernel,
        out_shape=jax.ShapeDtypeStruct((n, n), F32),
        in_specs=[pl.BlockSpec(memory_space=pltpu.VMEM)],
        out_specs=pl.BlockSpec(memory_space=pltpu.VMEM),
        scratch_shapes=[pltpu.VMEM((n, n), F32)],
        compiler_params=pltpu.CompilerParams(vmem_limit_bytes=16 << 20),
        cost_estimate=pl.CostEstimate(flops=1 << 30, bytes_accessed=1 << 20, transcendentals=0),
    )(c)


def gram_kernel(m_ref, out_ref, high, cross, low):
    step = pl.program_id(0)

    @pl.when(step == 0)
    def _():
        high[...] = jnp.zeros_like(high)
        cross[...] = jnp.zeros_like(cross)
        low[...] = jnp.zeros_like(low)

    h, l = split2(m_ref[...])
    high[...] += dot(h, h, 0, 0)
    cross[...] += dot(h, l, 0, 0)
    low[...] += dot(l, l, 0, 0)

    @pl.when(step == pl.num_programs(0) - 1)
    def _():
        c = cross[...]
        out_ref[...] = high[...] + (c + c.T + low[...])


def time_gram(field):
    rows, n = field.shape
    block = 1024
    return pl.pallas_call(
        gram_kernel,
        grid=(rows // block,),
        out_shape=jax.ShapeDtypeStruct((n, n), F32),
        in_specs=[pl.BlockSpec((block, n), lambda i: (i, 0))],
        out_specs=pl.BlockSpec((n, n), lambda i: (0, 0)),
        scratch_shapes=[pltpu.VMEM((n, n), F32)] * 3,
        compiler_params=pltpu.CompilerParams(vmem_limit_bytes=24 << 20),
    )(field)


def time_steps(g_ref, s_ref, gs):
    gs[0], gs[1], gs[2] = split3(g_ref[...])
    z0 = s_ref[...].T
    n = z0.shape[0]

    def apply_g(z):
        h, m, l = split3(z)
        a = dot(jnp.concatenate([h, m, l], axis=0), gs[0])
        b = dot(jnp.concatenate([h, m], axis=0), gs[1])
        c = dot(h, gs[2])
        return a[:n] + ((a[n : 2 * n] + b[:n]) + ((a[2 * n :] + b[n:]) + c))

    def gram(z):
        parts = jnp.concatenate(split3(z), axis=0)
        a = dot(parts, parts, 1, 1)
        two = a[:n, n : 2 * n] + a[n : 2 * n, :n]
        three = a[n : 2 * n, n : 2 * n] + (a[:n, 2 * n :] + a[2 * n :, :n])
        return a[:n, :n] + (two + three)

    def step(_, z):
        y = apply_g(z)
        inv = inverse_factor(gram(z))
        return dot(packed_lhs(split3(inv), 1), packed_rhs(split3(y)))

    z = lax.fori_loop(0, ITERS_T - 1, step, apply_g(z0))
    inv = inverse_factor(gram(z))
    return dot(packed_lhs(split3(inv), 1), packed_rhs(split3(z))).T


def project_kernel(g_ref, s_ref, u_ref, m_hbm, q_ref, shrunk_ref, v_ref, gs, m_left, m_right, weights, sems):
    rows, n = m_hbm.shape
    lanes = 128
    copies = [
        pltpu.make_async_copy(m_hbm.at[:, pl.ds(i * lanes, lanes)], half, sems.at[i])
        for i, half in enumerate((m_left, m_right))
    ]
    for copy in copies:
        copy.start()
    q = time_steps(g_ref, s_ref, gs)
    q_ref[...] = q
    rank = q.shape[1]
    per = lanes // rank
    qh, ql = split2(q)
    qh, ql = qh.astype(F32), ql.astype(F32)
    for k in range(per):
        pad = lambda a: jnp.pad(a, ((0, 0), (k * rank, lanes - (k + 1) * rank)))
        weights[k] = jnp.concatenate([pad(qh), pad(ql)], axis=1).astype(BF16)
    for copy in copies:
        copy.wait()
    cells_x = shrunk_ref.shape[0]
    cells_y = rows // cells_x
    for group in range(cells_y // per):
        wide = jnp.zeros((cells_x, 2 * lanes), F32)
        thin = jnp.zeros((cells_x, lanes), F32)
        for k in range(per):
            at = pl.ds(group * per + k, cells_x, stride=cells_y)
            h, l = split2(jnp.concatenate([m_left[at, :], m_right[at, :]], axis=1))
            wide = wide + dot(h, weights[k])
            thin = thin + dot(l, weights[k, :, :lanes])
        shrunk_ref[:, group * lanes : (group + 1) * lanes] = wide[:, :lanes] + (wide[:, lanes:] + thin)
    v_ref[...] = jnp.dot(u_ref[...].T, shrunk_ref[...], precision=HI, preferred_element_type=F32)


def project(gram, start_time, start_x, field, cells_x):
    rows, n = field.shape
    rank = start_time.shape[1]
    cols = rows // cells_x * rank
    vmem = pl.BlockSpec(memory_space=pltpu.VMEM)
    return pl.pallas_call(
        project_kernel,
        out_shape=(
            jax.ShapeDtypeStruct((n, rank), F32),
            jax.ShapeDtypeStruct((cells_x, cols), F32),
            jax.ShapeDtypeStruct((start_x.shape[1], cols), F32),
        ),
        in_specs=[vmem, vmem, vmem, pl.BlockSpec(memory_space=pl.ANY)],
        out_specs=(vmem, vmem, vmem),
        scratch_shapes=[
            pltpu.VMEM((3, n, n), BF16),
            pltpu.VMEM((rows, n // 2), F32),
            pltpu.VMEM((rows, n // 2), F32),
            pltpu.VMEM((128 // rank, n, 256), BF16),
            pltpu.SemaphoreType.DMA((2,)),
        ],
        compiler_params=pltpu.CompilerParams(vmem_limit_bytes=40 << 20),
    )(gram, start_time, start_x, field)


def precise(a, b, cb):
    return lax.dot_general(a, b, (((1,), (cb,)), ((), ())), precision=HI, preferred_element_type=F32)


def scatter_sum(v, axis, size):
    parts = v.reshape((size, v.shape[0] // size) + v.shape[1:])
    return jnp.sum(lax.all_to_all(parts, axis, 0, 0, tiled=True), axis=0)


def spread(p, axis, size):
    copies = jnp.broadcast_to(p[None], (size,) + p.shape)
    got = lax.all_to_all(copies, axis, 0, 0, tiled=True)
    return got.reshape((size * p.shape[0],) + p.shape[1:])


def sum_gy(z, size):
    ring = size // 2
    swap = [(2 * k + c, 2 * k + 1 - c) for k in range(ring) for c in range(2)]
    turn = lambda d: [(2 * k + c, 2 * ((k + d) % ring) + c) for k in range(ring) for c in range(2)]
    core = lax.axis_index("gy") % 2
    half = z.shape[0] // 2
    mine = lax.dynamic_slice_in_dim(z, core * half, half, 0)
    other = lax.dynamic_slice_in_dim(z, (1 - core) * half, half, 0)
    mine = mine + lax.ppermute(other, "gy", swap)
    total = (mine + lax.ppermute(mine, "gy", turn(2))) + (
        lax.ppermute(mine, "gy", turn(1)) + lax.ppermute(mine, "gy", turn(3))
    )
    rest = lax.ppermute(total, "gy", swap)
    first = core == 0
    return jnp.concatenate([jnp.where(first, total, rest), jnp.where(first, rest, total)], axis=0)


def local(melt_field, start_time, start_x, *, gx, gy):
    cells_x, cells_y, time_len = melt_field.shape
    field = melt_field.reshape(cells_x * cells_y, time_len)
    both = ("gx", "gy")
    gram = spread(scatter_sum(time_gram(field), both, gx * gy), both, gx * gy)
    time_basis, shrunk, v = project(gram, start_time, start_x, field, cells_x)
    cols = shrunk.shape[1]
    v = spread(scatter_sum(v, "gx", gx), "gx", gx)
    z = sum_gy(precise(v, shrunk, 1), gy)
    for sweep in range(SWEEPS_X - 1):
        vc = jnp.concatenate([precise(z, shrunk, 0), precise(z, z, 1)], axis=1)
        vc = spread(scatter_sum(vc, "gx", gx), "gx", gx)
        inv = chol_inverse(vc[:, cols:])
        z = precise(inv, sum_gy(precise(vc[:, :cols], shrunk, 1), gy), 0)
    inv = chol_inverse(spread(scatter_sum(precise(z, z, 1), "gx", gx), "gx", gx))
    u = precise(inv, z, 0)
    core = scatter_sum(precise(u, shrunk, 0), "gx", gx)
    return (time_basis, u.T, core)


def solution(mesh):
    in_specs = (P("gx", "gy", None), P(), P("gx", None))
    out_specs = (P(), P("gx", None), P("gx", "gy"))
    body = functools.partial(local, gx=mesh.shape["gx"], gy=mesh.shape["gy"])
    return jax.shard_map(body, mesh=mesh, in_specs=in_specs, out_specs=out_specs, check_vma=False)
```

```python
import functools

import jax
import jax.numpy as jnp
from jax import lax
from jax.experimental import pallas as pl
from jax.experimental.pallas import tpu as pltpu
from jax.sharding import PartitionSpec as P

ITERS_T = 8
SWEEPS_X = 3
F32 = jnp.float32
BF16 = jnp.bfloat16
HI = lax.Precision.HIGHEST


def split3(x):
    h = x.astype(BF16)
    rest = x - h.astype(F32)
    m = rest.astype(BF16)
    l = (rest - m.astype(F32)).astype(BF16)
    return h, m, l


def split2(x):
    h = x.astype(BF16)
    return h, (x - h.astype(F32)).astype(BF16)


def dot(a, b, ca=1, cb=0):
    return lax.dot_general(a, b, (((ca,), (cb,)), ((), ())), preferred_element_type=F32)


def inverse_factor(gram):
    n = gram.shape[0]
    tiles = n // 8
    left = [gram[8 * t : 8 * t + 8] for t in range(tiles)]
    row_id = lax.broadcasted_iota(jnp.int32, (8, n), 0)
    col_id = lax.broadcasted_iota(jnp.int32, (8, n), 1)
    right = [jnp.where(col_id == row_id + 8 * t, 1.0, 0.0).astype(F32) for t in range(tiles)]
    bc = lambda x, m: jnp.broadcast_to(x[m : m + 1], (8, n))
    lane = lambda x, j: jnp.broadcast_to(x[:, j : j + 1], (8, n))
    out = []
    cols = {(t, j): lane(left[t], j) for j in range(8) for t in range(tiles)}
    for b in range(tiles):
        for j in range(8 * b + 8, min(8 * b + 16, n)):
            for t in range(b + 1, tiles):
                cols[t, j] = lane(left[t], j)
        rows_l, rows_r = left[b], right[b]
        steps = []
        pivots = jnp.ones((8, n), F32)
        for m in range(0, 8, 2):
            c = 8 * b + m
            a, d, e = bc(cols[b, c], m), bc(cols[b, c + 1], m + 1), bc(cols[b, c + 1], m)
            ra = 1.0 / a
            ratio = e * ra
            rd = a * (1.0 / (a * d - e * e))
            pivots = jnp.where(row_id == m, a, jnp.where(row_id == m + 1, d - e * ratio, pivots))
            f0 = {t: cols[t, c] * ra for t in range(b, tiles)}
            f1 = {t: (cols[t, c + 1] - f0[t] * e) * rd for t in range(b, tiles)}
            f0[b] = jnp.where(row_id > m, f0[b], 0.0)
            f1[b] = jnp.where(row_id > m + 1, f1[b], 0.0)
            for j in range(c + 2, min(8 * b + 16, n)):
                tj, mj = j // 8, j % 8
                v0 = bc(cols[b, j], m) if tj == b else bc(cols[tj, c], mj)
                v1 = bc(cols[b, j], m + 1) if tj == b else bc(cols[tj, c + 1], mj)
                v1 = v1 - ratio * v0
                for t in range(tj, tiles):
                    cols[t, j] = (cols[t, j] - f0[t] * v0) - f1[t] * v1
            l0, r0 = bc(rows_l, m), bc(rows_r, m)
            l1, r1 = bc(rows_l, m + 1) - ratio * l0, bc(rows_r, m + 1) - ratio * r0
            rows_l = (rows_l - f0[b] * l0) - f1[b] * l1
            rows_r = (rows_r - f0[b] * r0) - f1[b] * r1
            steps += [(f0, l0, r0), (f1, l1, r1)]
        for t in range(b + 1, tiles):
            for factor, row_l, row_r in steps:
                left[t] = left[t] - factor[t] * row_l
                right[t] = right[t] - factor[t] * row_r
        out.append(rows_r * lax.rsqrt(pivots))
    return jnp.concatenate(out, axis=0)


def dot6(a, b, ca=1, cb=0):
    n = a.shape[0]
    h, m, l = split3(a)
    x = dot(jnp.concatenate([h, m, l], axis=0), b[0], ca, cb)
    y = dot(jnp.concatenate([h, m], axis=0), b[1], ca, cb)
    z = dot(h, b[2], ca, cb)
    return x[:n] + ((x[n : 2 * n] + y[:n]) + ((x[2 * n :] + y[n:]) + z))

def gram6(z):
    h, m, l = split3(z)
    a = jnp.concatenate([h, h, m, m, h, l], axis=1)
    b = jnp.concatenate([h, m, h, m, l, h], axis=1)
    return dot(a, b, 1, 1)


BLK = 32


def chol_kernel(c_ref, out_ref, work):
    n = c_ref.shape[0]
    col_id = lax.broadcasted_iota(jnp.int32, (BLK, n), 1)
    row_id = lax.broadcasted_iota(jnp.int32, (BLK, n), 0)
    work[...] = c_ref[...]
    diag = work[0:BLK, 0:BLK]
    for k in range(n // BLK):
        lo, hi = k * BLK, (k + 1) * BLK
        if hi < n:
            right = split3(work[lo:hi, hi : hi + BLK])
            below = work[hi : hi + BLK, lo:hi]
            after = work[hi : hi + BLK, hi : hi + BLK]
        in_blk = (col_id >= lo) & (col_id < hi)
        row = split3(jnp.where(in_blk, jnp.where(col_id - lo == row_id, 1.0, 0.0), work[lo:hi, :]))
        inv = inverse_factor(diag)
        if hi < n:
            panel = dot6(below, split3(inv), 1, 1)
            diag = after - dot6(panel, split3(dot6(inv, right)))
        r = dot6(inv, row)
        out_ref[lo:hi, :] = jnp.where(col_id < hi, r, 0.0)
        if hi < n:
            h, m, l = split3(r)
            xt = jnp.concatenate([h, h, m, m, h, l], axis=0)
            w = jnp.concatenate([h, m, h, m, l, h], axis=0)
            base = hi // 128 * 128
            upd = dot(xt[:, base:], w, 0, 0)
            cid = lax.broadcasted_iota(jnp.int32, (n - hi, n), 1)
            old = jnp.where((cid >= lo) & (cid < hi), 0.0, work[hi:, :])
            work[hi:, :] = old - upd[hi - base :, :]


def chol_inverse(c):
    n = c.shape[0]
    return pl.pallas_call(
        chol_kernel,
        out_shape=jax.ShapeDtypeStruct((n, n), F32),
        in_specs=[pl.BlockSpec(memory_space=pltpu.VMEM)],
        out_specs=pl.BlockSpec(memory_space=pltpu.VMEM),
        scratch_shapes=[pltpu.VMEM((n, n), F32)],
        compiler_params=pltpu.CompilerParams(vmem_limit_bytes=16 << 20),
        cost_estimate=pl.CostEstimate(flops=1 << 30, bytes_accessed=1 << 20, transcendentals=0),
    )(c)


def gram_kernel(m_ref, out_ref, high, cross, low):
    step = pl.program_id(0)

    @pl.when(step == 0)
    def _():
        high[...] = jnp.zeros_like(high)
        cross[...] = jnp.zeros_like(cross)
        low[...] = jnp.zeros_like(low)

    h, l = split2(m_ref[...])
    high[...] += dot(h, h, 0, 0)
    cross[...] += dot(h, l, 0, 0)
    low[...] += dot(l, l, 0, 0)

    @pl.when(step == pl.num_programs(0) - 1)
    def _():
        c = cross[...]
        out_ref[...] = high[...] + (c + c.T + low[...])


def time_gram(field):
    rows, n = field.shape
    block = 1024
    return pl.pallas_call(
        gram_kernel,
        grid=(rows // block,),
        out_shape=jax.ShapeDtypeStruct((n, n), F32),
        in_specs=[pl.BlockSpec((block, n), lambda i: (i, 0))],
        out_specs=pl.BlockSpec((n, n), lambda i: (0, 0)),
        scratch_shapes=[pltpu.VMEM((n, n), F32)] * 3,
        compiler_params=pltpu.CompilerParams(vmem_limit_bytes=56 << 20),
    )(field)


def time_steps(g_ref, s_ref, gs):
    gs[0], gs[1], gs[2] = split3(g_ref[...])

    def apply_g(z):
        return dot6(z, (gs[0], gs[1], gs[2]))

    def step(_, z):
        y = apply_g(z)
        return dot6(inverse_factor(gram6(z)), split3(y))

    z = lax.fori_loop(0, ITERS_T - 1, step, apply_g(s_ref[...].T))
    return dot6(inverse_factor(gram6(z)), split3(z)).T


def project_kernel(g_ref, s_ref, u_ref, m_hbm, q_ref, shrunk_ref, v_ref, gs, m_left, m_right, weights, sems):
    rows, n = m_hbm.shape
    lanes = 128
    copies = [
        pltpu.make_async_copy(m_hbm.at[:, pl.ds(i * lanes, lanes)], half, sems.at[i])
        for i, half in enumerate((m_left, m_right))
    ]
    for copy in copies:
        copy.start()
    q = time_steps(g_ref, s_ref, gs)
    q_ref[...] = q
    rank = q.shape[1]
    per = lanes // rank
    qh, ql = split2(q)
    qh, ql = qh.astype(F32), ql.astype(F32)
    for k in range(per):
        pad = lambda a: jnp.pad(a, ((0, 0), (k * rank, lanes - (k + 1) * rank)))
        weights[k] = jnp.concatenate([pad(qh), pad(ql)], axis=1).astype(BF16)
    for copy in copies:
        copy.wait()
    cells_x = shrunk_ref.shape[0]
    cells_y = rows // cells_x
    for group in range(cells_y // per):
        wide = jnp.zeros((cells_x, 2 * lanes), F32)
        thin = jnp.zeros((cells_x, lanes), F32)
        for k in range(per):
            at = pl.ds(group * per + k, cells_x, stride=cells_y)
            h, l = split2(jnp.concatenate([m_left[at, :], m_right[at, :]], axis=1))
            wide = wide + dot(h, weights[k])
            thin = thin + dot(l, weights[k, :, :lanes])
        shrunk_ref[:, group * lanes : (group + 1) * lanes] = wide[:, :lanes] + (wide[:, lanes:] + thin)
    v_ref[...] = jnp.dot(u_ref[...].T, shrunk_ref[...], precision=HI, preferred_element_type=F32)


def project(gram, start_time, start_x, field, cells_x):
    rows, n = field.shape
    rank = start_time.shape[1]
    cols = rows // cells_x * rank
    vmem = pl.BlockSpec(memory_space=pltpu.VMEM)
    return pl.pallas_call(
        project_kernel,
        out_shape=(
            jax.ShapeDtypeStruct((n, rank), F32),
            jax.ShapeDtypeStruct((cells_x, cols), F32),
            jax.ShapeDtypeStruct((start_x.shape[1], cols), F32),
        ),
        in_specs=[vmem, vmem, vmem, pl.BlockSpec(memory_space=pl.ANY)],
        out_specs=(vmem, vmem, vmem),
        scratch_shapes=[
            pltpu.VMEM((3, n, n), BF16),
            pltpu.VMEM((rows, n // 2), F32),
            pltpu.VMEM((rows, n // 2), F32),
            pltpu.VMEM((128 // rank, n, 256), BF16),
            pltpu.SemaphoreType.DMA((2,)),
        ],
        compiler_params=pltpu.CompilerParams(vmem_limit_bytes=56 << 20),
    )(gram, start_time, start_x, field)


def precise(a, b, cb):
    return lax.dot_general(a, b, (((1,), (cb,)), ((), ())), precision=HI, preferred_element_type=F32)


def scatter_sum(v, axis, size):
    parts = v.reshape((size, v.shape[0] // size) + v.shape[1:])
    return jnp.sum(lax.all_to_all(parts, axis, 0, 0, tiled=True), axis=0)


def spread(p, axis, size):
    copies = jnp.broadcast_to(p[None], (size,) + p.shape)
    got = lax.all_to_all(copies, axis, 0, 0, tiled=True)
    return got.reshape((size * p.shape[0],) + p.shape[1:])


def gy_moves(size):
    ring = size // 2
    swap = [(2 * k + c, 2 * k + 1 - c) for k in range(ring) for c in range(2)]
    turns = [[(2 * k + c, 2 * ((k + d) % ring) + c) for k in range(ring) for c in range(2)] for d in (1, 2, 3)]
    return swap, turns


def sum_gy_small(p, size):
    swap, turns = gy_moves(size)
    p = p + lax.ppermute(p, "gy", swap)
    got = [lax.ppermute(p, "gy", turn) for turn in turns]
    return (p + got[1]) + (got[0] + got[2])


def sum_gy(z, size, square=None):
    swap, turns = gy_moves(size)
    core = lax.axis_index("gy") % 2
    half = z.shape[0] // 2
    mine = lax.dynamic_slice_in_dim(z, core * half, half, 0)
    other = lax.dynamic_slice_in_dim(z, (1 - core) * half, half, 0)
    mine = mine + lax.ppermute(other, "gy", swap)
    inv = None
    if square is not None:
        mine, square = lax.optimization_barrier((mine, square))
    got = [lax.ppermute(mine, "gy", turn) for turn in turns]
    if square is not None:
        got, inv = lax.optimization_barrier((got, chol_inverse(square)))
    total = (mine + got[1]) + (got[0] + got[2])
    rest = lax.ppermute(total, "gy", swap)
    first = core == 0
    full = jnp.concatenate([jnp.where(first, total, rest), jnp.where(first, rest, total)], axis=0)
    return full, inv


def local(melt_field, start_time, start_x, *, gx, gy):
    cells_x, cells_y, time_len = melt_field.shape
    field = melt_field.reshape(cells_x * cells_y, time_len)
    gram = spread(sum_gy_small(scatter_sum(time_gram(field), "gx", gx), gy), "gx", gx)
    time_basis, shrunk, v = project(gram, start_time, start_x, field, cells_x)
    cols = shrunk.shape[1]
    v = spread(scatter_sum(v, "gx", gx), "gx", gx)
    z, _ = sum_gy(precise(v, shrunk, 1), gy)
    for sweep in range(SWEEPS_X - 1):
        vc = jnp.concatenate([precise(z, shrunk, 0), precise(z, z, 1)], axis=1)
        vc = spread(scatter_sum(vc, "gx", gx), "gx", gx)
        z, inv = sum_gy(precise(vc[:, :cols], shrunk, 1), gy, vc[:, cols:])
        z = precise(inv, z, 0)
    inv = chol_inverse(spread(scatter_sum(precise(z, z, 1), "gx", gx), "gx", gx))
    u = precise(inv, z, 0)
    core = scatter_sum(precise(u, shrunk, 0), "gx", gx)
    return (time_basis, u.T, core)


def solution(mesh):
    in_specs = (P("gx", "gy", None), P(), P("gx", None))
    out_specs = (P(), P("gx", None), P("gx", "gy"))
    body = functools.partial(local, gx=mesh.shape["gx"], gy=mesh.shape["gy"])
    return jax.shard_map(body, mesh=mesh, in_specs=in_specs, out_specs=out_specs, check_vma=False)
```

```python
import functools

import jax
import jax.numpy as jnp
from jax import lax
from jax.experimental import pallas as pl
from jax.experimental.pallas import tpu as pltpu
from jax.sharding import PartitionSpec as P

ITERS_T = 8
SWEEPS_X = 3
F32 = jnp.float32
BF16 = jnp.bfloat16
HI = lax.Precision.HIGHEST


def split3(x):
    h = x.astype(BF16)
    rest = x - h.astype(F32)
    m = rest.astype(BF16)
    l = (rest - m.astype(F32)).astype(BF16)
    return h, m, l


def split2(x):
    h = x.astype(BF16)
    return h, (x - h.astype(F32)).astype(BF16)


def dot(a, b, ca=1, cb=0):
    return lax.dot_general(a, b, (((ca,), (cb,)), ((), ())), preferred_element_type=F32)


def inverse_factor(gram):
    n = gram.shape[0]
    tiles = n // 8
    left = [gram[8 * t : 8 * t + 8] for t in range(tiles)]
    row_id = lax.broadcasted_iota(jnp.int32, (8, n), 0)
    col_id = lax.broadcasted_iota(jnp.int32, (8, n), 1)
    right = [jnp.where(col_id == row_id + 8 * t, 1.0, 0.0).astype(F32) for t in range(tiles)]
    bc = lambda x, m: jnp.broadcast_to(x[m : m + 1], (8, n))
    lane = lambda x, j: jnp.broadcast_to(x[:, j : j + 1], (8, n))
    out = []
    cols = {(t, j): lane(left[t], j) for j in range(8) for t in range(tiles)}
    for b in range(tiles):
        for j in range(8 * b + 8, min(8 * b + 16, n)):
            for t in range(b + 1, tiles):
                cols[t, j] = lane(left[t], j)
        rows_l, rows_r = left[b], right[b]
        steps = []
        pivots = jnp.ones((8, n), F32)
        for m in range(0, 8, 2):
            c = 8 * b + m
            a, d, e = bc(cols[b, c], m), bc(cols[b, c + 1], m + 1), bc(cols[b, c + 1], m)
            ra = 1.0 / a
            ratio = e * ra
            rd = a * (1.0 / (a * d - e * e))
            pivots = jnp.where(row_id == m, a, jnp.where(row_id == m + 1, d - e * ratio, pivots))
            f0 = {t: cols[t, c] * ra for t in range(b, tiles)}
            f1 = {t: (cols[t, c + 1] - f0[t] * e) * rd for t in range(b, tiles)}
            f0[b] = jnp.where(row_id > m, f0[b], 0.0)
            f1[b] = jnp.where(row_id > m + 1, f1[b], 0.0)
            for j in range(c + 2, min(8 * b + 16, n)):
                tj, mj = j // 8, j % 8
                v0 = bc(cols[b, j], m) if tj == b else bc(cols[tj, c], mj)
                v1 = bc(cols[b, j], m + 1) if tj == b else bc(cols[tj, c + 1], mj)
                v1 = v1 - ratio * v0
                for t in range(tj, tiles):
                    cols[t, j] = (cols[t, j] - f0[t] * v0) - f1[t] * v1
            l0, r0 = bc(rows_l, m), bc(rows_r, m)
            l1, r1 = bc(rows_l, m + 1) - ratio * l0, bc(rows_r, m + 1) - ratio * r0
            rows_l = (rows_l - f0[b] * l0) - f1[b] * l1
            rows_r = (rows_r - f0[b] * r0) - f1[b] * r1
            steps += [(f0, l0, r0), (f1, l1, r1)]
        for t in range(b + 1, tiles):
            for factor, row_l, row_r in steps:
                left[t] = left[t] - factor[t] * row_l
                right[t] = right[t] - factor[t] * row_r
        out.append(rows_r * lax.rsqrt(pivots))
    return jnp.concatenate(out, axis=0)


def dot6(a, b, ca=1, cb=0):
    n = a.shape[0]
    h, m, l = split3(a)
    x = dot(jnp.concatenate([h, m, l], axis=0), b[0], ca, cb)
    y = dot(jnp.concatenate([h, m], axis=0), b[1], ca, cb)
    z = dot(h, b[2], ca, cb)
    return x[:n] + ((x[n : 2 * n] + y[:n]) + ((x[2 * n :] + y[n:]) + z))

def gram6(z):
    h, m, l = split3(z)
    a = jnp.concatenate([h, h, m, m, h, l], axis=1)
    b = jnp.concatenate([h, m, h, m, l, h], axis=1)
    return dot(a, b, 1, 1)


BLK = 32


def chol_kernel(c_ref, out_ref, work):
    n = c_ref.shape[0]
    col_id = lax.broadcasted_iota(jnp.int32, (BLK, n), 1)
    row_id = lax.broadcasted_iota(jnp.int32, (BLK, n), 0)
    work[...] = c_ref[...]
    diag = work[0:BLK, 0:BLK]
    for k in range(n // BLK):
        lo, hi = k * BLK, (k + 1) * BLK
        if hi < n:
            right = split3(work[lo:hi, hi : hi + BLK])
            below = work[hi : hi + BLK, lo:hi]
            after = work[hi : hi + BLK, hi : hi + BLK]
        in_blk = (col_id >= lo) & (col_id < hi)
        row = split3(jnp.where(in_blk, jnp.where(col_id - lo == row_id, 1.0, 0.0), work[lo:hi, :]))
        inv = inverse_factor(diag)
        if hi < n:
            panel = dot6(below, split3(inv), 1, 1)
            diag = after - dot6(panel, split3(dot6(inv, right)))
        r = dot6(inv, row)
        out_ref[lo:hi, :] = jnp.where(col_id < hi, r, 0.0)
        if hi < n:
            h, m, l = split3(r)
            xt = jnp.concatenate([h, h, m, m, h, l], axis=0)
            w = jnp.concatenate([h, m, h, m, l, h], axis=0)
            base = hi // 128 * 128
            upd = dot(xt[:, base:], w, 0, 0)
            cid = lax.broadcasted_iota(jnp.int32, (n - hi, n), 1)
            old = jnp.where((cid >= lo) & (cid < hi), 0.0, work[hi:, :])
            work[hi:, :] = old - upd[hi - base :, :]


def chol_inverse(c):
    n = c.shape[0]
    return pl.pallas_call(
        chol_kernel,
        out_shape=jax.ShapeDtypeStruct((n, n), F32),
        in_specs=[pl.BlockSpec(memory_space=pltpu.VMEM)],
        out_specs=pl.BlockSpec(memory_space=pltpu.VMEM),
        scratch_shapes=[pltpu.VMEM((n, n), F32)],
        compiler_params=pltpu.CompilerParams(vmem_limit_bytes=16 << 20),
        cost_estimate=pl.CostEstimate(flops=1 << 30, bytes_accessed=1 << 20, transcendentals=0),
    )(c)


CHUNKS = (512, 1536, 2048, 2048, 2048)


def gram_kernel(m_hbm, out_ref, buf, sems):
    copies, starts, at = [], [], 0
    for i, rows in enumerate(CHUNKS):
        span = pl.ds(at, rows)
        copies.append(pltpu.make_async_copy(m_hbm.at[span], buf.at[span], sems.at[i]))
        starts.append(at)
        at += rows
    for copy in copies:
        copy.start()
    high = cross = low = None
    for copy, at, rows in zip(copies, starts, CHUNKS):
        copy.wait()
        h, l = split2(buf[at : at + rows, :])
        hh, hl, ll = dot(h, h, 0, 0), dot(h, l, 0, 0), dot(l, l, 0, 0)
        high, cross, low = (hh, hl, ll) if high is None else (high + hh, cross + hl, low + ll)
    out_ref[...] = high + (cross + cross.T + low)


def time_gram(field):
    n = field.shape[1]
    assert field.shape[0] == sum(CHUNKS)
    return pl.pallas_call(
        gram_kernel,
        out_shape=jax.ShapeDtypeStruct((n, n), F32),
        in_specs=[pl.BlockSpec(memory_space=pl.ANY)],
        out_specs=pl.BlockSpec(memory_space=pltpu.VMEM),
        scratch_shapes=[pltpu.VMEM(field.shape, F32), pltpu.SemaphoreType.DMA((len(CHUNKS),))],
        compiler_params=pltpu.CompilerParams(vmem_limit_bytes=56 << 20),
    )(field)


def time_steps(g_ref, s_ref, gs):
    gs[0], gs[1], gs[2] = split3(g_ref[...])

    def apply_g(z):
        return dot6(z, (gs[0], gs[1], gs[2]))

    def step(_, z):
        y = apply_g(z)
        return dot6(inverse_factor(gram6(z)), split3(y))

    z = lax.fori_loop(0, ITERS_T - 1, step, apply_g(s_ref[...].T))
    return dot6(inverse_factor(gram6(z)), split3(z)).T


def project_kernel(g_ref, s_ref, u_ref, m_hbm, q_ref, shrunk_ref, v_ref, gs, by_y, weights, sems):
    cells_y = m_hbm.shape[1]
    lanes = 128
    copies = [pltpu.make_async_copy(m_hbm.at[:, y, :], by_y.at[y], sems.at[y]) for y in range(cells_y)]
    for copy in copies:
        copy.start()
    q = time_steps(g_ref, s_ref, gs)
    q_ref[...] = q
    rank = q.shape[1]
    per = lanes // rank
    qh, ql = split2(q)
    qh, ql = qh.astype(F32), ql.astype(F32)
    for k in range(per):
        pad = lambda a: jnp.pad(a, ((0, 0), (k * rank, lanes - (k + 1) * rank)))
        weights[k] = jnp.concatenate([pad(qh), pad(ql)], axis=1).astype(BF16)
    for group in range(cells_y // per):
        wide = thin = None
        for k in range(per):
            y = group * per + k
            copies[y].wait()
            h, l = split2(by_y[y])
            a, b = dot(h, weights[k]), dot(l, weights[k, :, :lanes])
            wide, thin = (a, b) if k == 0 else (wide + a, thin + b)
        shrunk_ref[:, group * lanes : (group + 1) * lanes] = wide[:, :lanes] + (wide[:, lanes:] + thin)
    v_ref[...] = jnp.dot(u_ref[...].T, shrunk_ref[...], precision=HI, preferred_element_type=F32)


def project(gram, start_time, start_x, field):
    cells_x, cells_y, n = field.shape
    rank = start_time.shape[1]
    cols = cells_y * rank
    vmem = pl.BlockSpec(memory_space=pltpu.VMEM)
    return pl.pallas_call(
        project_kernel,
        out_shape=(
            jax.ShapeDtypeStruct((n, rank), F32),
            jax.ShapeDtypeStruct((cells_x, cols), F32),
            jax.ShapeDtypeStruct((start_x.shape[1], cols), F32),
        ),
        in_specs=[vmem, vmem, vmem, pl.BlockSpec(memory_space=pl.ANY)],
        out_specs=(vmem, vmem, vmem),
        scratch_shapes=[
            pltpu.VMEM((3, n, n), BF16),
            pltpu.VMEM((cells_y, cells_x, n), F32),
            pltpu.VMEM((128 // rank, n, 256), BF16),
            pltpu.SemaphoreType.DMA((cells_y,)),
        ],
        compiler_params=pltpu.CompilerParams(vmem_limit_bytes=56 << 20),
    )(gram, start_time, start_x, field)


def precise(a, b, cb):
    return lax.dot_general(a, b, (((1,), (cb,)), ((), ())), precision=HI, preferred_element_type=F32)


def scatter_sum(v, axis, size):
    parts = v.reshape((size, v.shape[0] // size) + v.shape[1:])
    return jnp.sum(lax.all_to_all(parts, axis, 0, 0, tiled=True), axis=0)


def spread(p, axis, size):
    copies = jnp.broadcast_to(p[None], (size,) + p.shape)
    got = lax.all_to_all(copies, axis, 0, 0, tiled=True)
    return got.reshape((size * p.shape[0],) + p.shape[1:])


def gy_moves(size):
    ring = size // 2
    swap = [(2 * k + c, 2 * k + 1 - c) for k in range(ring) for c in range(2)]
    turns = [[(2 * k + c, 2 * ((k + d) % ring) + c) for k in range(ring) for c in range(2)] for d in (1, 2, 3)]
    return swap, turns


def sum_gy_small(p, size):
    swap, turns = gy_moves(size)
    p = p + lax.ppermute(p, "gy", swap)
    got = [lax.ppermute(p, "gy", turn) for turn in turns]
    return (p + got[1]) + (got[0] + got[2])


def both_halves(mine, size):
    rest = lax.ppermute(mine, "gy", gy_moves(size)[0])
    first = lax.axis_index("gy") % 2 == 0
    return jnp.concatenate([jnp.where(first, mine, rest), jnp.where(first, rest, mine)], axis=0)


def sum_gy(part, size, square=None):
    inv = None
    if square is not None:
        part, square = lax.optimization_barrier((part, square))
    got = [lax.ppermute(part, "gy", turn) for turn in gy_moves(size)[1]]
    if square is not None:
        got, inv = lax.optimization_barrier((got, chol_inverse(square)))
    return both_halves((part + got[1]) + (got[0] + got[2]), size), inv


def local(melt_field, start_time, start_x, *, gx, gy):
    cells_x, cells_y, time_len = melt_field.shape
    field = melt_field.reshape(cells_x * cells_y, time_len)
    gram = spread(sum_gy_small(scatter_sum(time_gram(field), "gx", gx), gy), "gx", gx)
    core_id = lax.axis_index("gy") % 2
    half = start_x.shape[1] // 2
    start = lax.dynamic_slice_in_dim(start_x, core_id * half, half, 1)
    time_basis, own, v = project(gram, start_time, start, melt_field)
    other = lax.ppermute(own, "gy", gy_moves(gy)[0])
    v = jnp.concatenate([v, precise(start.T, other, 0)], axis=1)
    chip = jnp.concatenate([own, other], axis=1)
    cols = chip.shape[1]
    v = spread(scatter_sum(v, "gx", gx), "gx", gx)
    z, _ = sum_gy(precise(v, chip, 1), gy)
    for sweep in range(SWEEPS_X - 1):
        mine = lax.dynamic_slice_in_dim(z, core_id * half, half, 0)
        vc = jnp.concatenate([precise(mine, chip, 0), precise(mine, z, 1)], axis=1)
        vc = spread(scatter_sum(vc, "gx", gx), "gx", gx)
        square = both_halves(vc[:, cols:], gy)
        z, inv = sum_gy(precise(vc[:, :cols], chip, 1), gy, square)
        z = precise(inv, z, 0)
    inv = chol_inverse(spread(scatter_sum(precise(z, z, 1), "gx", gx), "gx", gx))
    u = precise(inv, z, 0)
    core = scatter_sum(precise(u, own, 0), "gx", gx)
    return (time_basis, u.T, core)


def solution(mesh):
    in_specs = (P("gx", "gy", None), P(), P("gx", None))
    out_specs = (P(), P("gx", None), P("gx", "gy"))
    body = functools.partial(local, gx=mesh.shape["gx"], gy=mesh.shape["gy"])
    return jax.shard_map(body, mesh=mesh, in_specs=in_specs, out_specs=out_specs, check_vma=False)
```

```python
import functools

import jax
import jax.numpy as jnp
from jax import lax
from jax.experimental import pallas as pl
from jax.experimental.pallas import tpu as pltpu
from jax.sharding import PartitionSpec as P

ITERS_T = 8
SWEEPS_X = 3
F32 = jnp.float32
BF16 = jnp.bfloat16
HI = lax.Precision.HIGHEST


def split3(x):
    h = x.astype(BF16)
    rest = x - h.astype(F32)
    m = rest.astype(BF16)
    l = (rest - m.astype(F32)).astype(BF16)
    return h, m, l


def split2(x):
    h = x.astype(BF16)
    return h, (x - h.astype(F32)).astype(BF16)


def dot(a, b, ca=1, cb=0):
    return lax.dot_general(a, b, (((ca,), (cb,)), ((), ())), preferred_element_type=F32)


def inverse_factor(gram):
    n = gram.shape[0]
    tiles = n // 8
    left = [gram[8 * t : 8 * t + 8] for t in range(tiles)]
    row_id = lax.broadcasted_iota(jnp.int32, (8, n), 0)
    col_id = lax.broadcasted_iota(jnp.int32, (8, n), 1)
    right = [jnp.where(col_id == row_id + 8 * t, 1.0, 0.0).astype(F32) for t in range(tiles)]
    bc = lambda x, m: jnp.broadcast_to(x[m : m + 1], (8, n))
    lane = lambda x, j: jnp.broadcast_to(x[:, j : j + 1], (8, n))
    out = []
    cols = {(t, j): lane(left[t], j) for j in range(8) for t in range(tiles)}
    for b in range(tiles):
        for j in range(8 * b + 8, min(8 * b + 16, n)):
            for t in range(b + 1, tiles):
                cols[t, j] = lane(left[t], j)
        rows_l, rows_r = left[b], right[b]
        steps = []
        pivots = jnp.ones((8, n), F32)
        for m in range(0, 8, 2):
            c = 8 * b + m
            a, d, e = bc(cols[b, c], m), bc(cols[b, c + 1], m + 1), bc(cols[b, c + 1], m)
            ra = 1.0 / a
            ratio = e * ra
            rd = a * (1.0 / (a * d - e * e))
            pivots = jnp.where(row_id == m, a, jnp.where(row_id == m + 1, d - e * ratio, pivots))
            f0 = {t: cols[t, c] * ra for t in range(b, tiles)}
            f1 = {t: (cols[t, c + 1] - f0[t] * e) * rd for t in range(b, tiles)}
            f0[b] = jnp.where(row_id > m, f0[b], 0.0)
            f1[b] = jnp.where(row_id > m + 1, f1[b], 0.0)
            for j in range(c + 2, min(8 * b + 16, n)):
                tj, mj = j // 8, j % 8
                v0 = bc(cols[b, j], m) if tj == b else bc(cols[tj, c], mj)
                v1 = bc(cols[b, j], m + 1) if tj == b else bc(cols[tj, c + 1], mj)
                v1 = v1 - ratio * v0
                for t in range(tj, tiles):
                    cols[t, j] = (cols[t, j] - f0[t] * v0) - f1[t] * v1
            l0, r0 = bc(rows_l, m), bc(rows_r, m)
            l1, r1 = bc(rows_l, m + 1) - ratio * l0, bc(rows_r, m + 1) - ratio * r0
            rows_l = (rows_l - f0[b] * l0) - f1[b] * l1
            rows_r = (rows_r - f0[b] * r0) - f1[b] * r1
            steps += [(f0, l0, r0), (f1, l1, r1)]
        for t in range(b + 1, tiles):
            for factor, row_l, row_r in steps:
                left[t] = left[t] - factor[t] * row_l
                right[t] = right[t] - factor[t] * row_r
        out.append(rows_r * lax.rsqrt(pivots))
    return jnp.concatenate(out, axis=0)


def dot6(a, b, ca=1, cb=0):
    n = a.shape[0]
    h, m, l = split3(a)
    x = dot(jnp.concatenate([h, m, l], axis=0), b[0], ca, cb)
    y = dot(jnp.concatenate([h, m], axis=0), b[1], ca, cb)
    z = dot(h, b[2], ca, cb)
    return x[:n] + ((x[n : 2 * n] + y[:n]) + ((x[2 * n :] + y[n:]) + z))

def gram6(z):
    h, m, l = split3(z)
    a = jnp.concatenate([h, h, m, m, h, l], axis=1)
    b = jnp.concatenate([h, m, h, m, l, h], axis=1)
    return dot(a, b, 1, 1)


BLK = 32


def chol_kernel(c_ref, out_ref, work):
    n = c_ref.shape[0]
    col_id = lax.broadcasted_iota(jnp.int32, (BLK, n), 1)
    row_id = lax.broadcasted_iota(jnp.int32, (BLK, n), 0)
    work[...] = c_ref[...]
    diag = work[0:BLK, 0:BLK]
    for k in range(n // BLK):
        lo, hi = k * BLK, (k + 1) * BLK
        if hi < n:
            right = split3(work[lo:hi, hi : hi + BLK])
            below = work[hi : hi + BLK, lo:hi]
            after = work[hi : hi + BLK, hi : hi + BLK]
        in_blk = (col_id >= lo) & (col_id < hi)
        row = split3(jnp.where(in_blk, jnp.where(col_id - lo == row_id, 1.0, 0.0), work[lo:hi, :]))
        inv = inverse_factor(diag)
        if hi < n:
            panel = dot6(below, split3(inv), 1, 1)
            diag = after - dot6(panel, split3(dot6(inv, right)))
        r = dot6(inv, row)
        out_ref[lo:hi, :] = jnp.where(col_id < hi, r, 0.0)
        if hi < n:
            h, m, l = split3(r)
            xt = jnp.concatenate([h, h, m, m, h, l], axis=0)
            w = jnp.concatenate([h, m, h, m, l, h], axis=0)
            base = hi // 128 * 128
            upd = dot(xt[:, base:], w, 0, 0)
            cid = lax.broadcasted_iota(jnp.int32, (n - hi, n), 1)
            old = jnp.where((cid >= lo) & (cid < hi), 0.0, work[hi:, :])
            work[hi:, :] = old - upd[hi - base :, :]


def chol_inverse(c):
    n = c.shape[0]
    return pl.pallas_call(
        chol_kernel,
        out_shape=jax.ShapeDtypeStruct((n, n), F32),
        in_specs=[pl.BlockSpec(memory_space=pltpu.VMEM)],
        out_specs=pl.BlockSpec(memory_space=pltpu.VMEM),
        scratch_shapes=[pltpu.VMEM((n, n), F32)],
        compiler_params=pltpu.CompilerParams(vmem_limit_bytes=16 << 20),
        cost_estimate=pl.CostEstimate(flops=1 << 30, bytes_accessed=1 << 20, transcendentals=0),
    )(c)


CHUNKS = (512, 1536, 2048, 2048, 2048)


def gram_kernel(m_hbm, out_ref, buf, sems):
    copies, starts, at = [], [], 0
    for i, rows in enumerate(CHUNKS):
        span = pl.ds(at, rows)
        copies.append(pltpu.make_async_copy(m_hbm.at[span], buf.at[span], sems.at[i]))
        starts.append(at)
        at += rows
    for copy in copies:
        copy.start()
    high = cross = low = None
    for copy, at, rows in zip(copies, starts, CHUNKS):
        copy.wait()
        h, l = split2(buf[at : at + rows, :])
        hh, hl, ll = dot(h, h, 0, 0), dot(h, l, 0, 0), dot(l, l, 0, 0)
        high, cross, low = (hh, hl, ll) if high is None else (high + hh, cross + hl, low + ll)
    out_ref[...] = high + (cross + cross.T + low)


def time_gram(field):
    n = field.shape[1]
    assert field.shape[0] == sum(CHUNKS)
    return pl.pallas_call(
        gram_kernel,
        out_shape=jax.ShapeDtypeStruct((n, n), F32),
        in_specs=[pl.BlockSpec(memory_space=pl.ANY)],
        out_specs=pl.BlockSpec(memory_space=pltpu.VMEM),
        scratch_shapes=[pltpu.VMEM(field.shape, F32), pltpu.SemaphoreType.DMA((len(CHUNKS),))],
        compiler_params=pltpu.CompilerParams(vmem_limit_bytes=56 << 20),
    )(field)


def time_steps(g_ref, s_ref, gs):
    gs[0], gs[1], gs[2] = split3(g_ref[...])

    def apply_g(z):
        return dot6(z, (gs[0], gs[1], gs[2]))

    def step(_, z):
        y = apply_g(z)
        return dot6(inverse_factor(gram6(z)), split3(y))

    z = lax.fori_loop(0, ITERS_T - 1, step, apply_g(s_ref[...].T))
    return dot6(inverse_factor(gram6(z)), split3(z)).T


def project_kernel(g_ref, s_ref, u_ref, m_hbm, q_ref, shrunk_ref, v_ref, gs, by_y, weights, sems):
    cells_y = m_hbm.shape[1]
    lanes = 128
    copies = [pltpu.make_async_copy(m_hbm.at[:, y, :], by_y.at[y], sems.at[y]) for y in range(cells_y)]
    for copy in copies:
        copy.start()
    q = time_steps(g_ref, s_ref, gs)
    q_ref[...] = q
    rank = q.shape[1]
    per = lanes // rank
    qh, ql = split2(q)
    qh, ql = qh.astype(F32), ql.astype(F32)
    for k in range(per):
        pad = lambda a: jnp.pad(a, ((0, 0), (k * rank, lanes - (k + 1) * rank)))
        weights[k] = jnp.concatenate([pad(qh), pad(ql)], axis=1).astype(BF16)
    for copy in copies:
        copy.wait()
    for group in range(cells_y // per):
        wide = thin = None
        for k in range(per):
            h, l = split2(by_y[group * per + k])
            a, b = dot(h, weights[k]), dot(l, weights[k, :, :lanes])
            wide, thin = (a, b) if k == 0 else (wide + a, thin + b)
        shrunk_ref[:, group * lanes : (group + 1) * lanes] = wide[:, :lanes] + (wide[:, lanes:] + thin)
    v_ref[...] = jnp.dot(u_ref[...].T, shrunk_ref[...], precision=HI, preferred_element_type=F32)


def project(gram, start_time, start_x, field):
    cells_x, cells_y, n = field.shape
    rank = start_time.shape[1]
    cols = cells_y * rank
    vmem = pl.BlockSpec(memory_space=pltpu.VMEM)
    return pl.pallas_call(
        project_kernel,
        out_shape=(
            jax.ShapeDtypeStruct((n, rank), F32),
            jax.ShapeDtypeStruct((cells_x, cols), F32),
            jax.ShapeDtypeStruct((start_x.shape[1], cols), F32),
        ),
        in_specs=[vmem, vmem, vmem, pl.BlockSpec(memory_space=pl.ANY)],
        out_specs=(vmem, vmem, vmem),
        scratch_shapes=[
            pltpu.VMEM((3, n, n), BF16),
            pltpu.VMEM((cells_y, cells_x, n), F32),
            pltpu.VMEM((128 // rank, n, 256), BF16),
            pltpu.SemaphoreType.DMA((cells_y,)),
        ],
        compiler_params=pltpu.CompilerParams(vmem_limit_bytes=56 << 20),
    )(gram, start_time, start_x, field)


def precise(a, b, cb):
    return lax.dot_general(a, b, (((1,), (cb,)), ((), ())), precision=HI, preferred_element_type=F32)


def scatter_sum(v, axis, size):
    parts = v.reshape((size, v.shape[0] // size) + v.shape[1:])
    return jnp.sum(lax.all_to_all(parts, axis, 0, 0, tiled=True), axis=0)


def spread(p, axis, size):
    copies = jnp.broadcast_to(p[None], (size,) + p.shape)
    got = lax.all_to_all(copies, axis, 0, 0, tiled=True)
    return got.reshape((size * p.shape[0],) + p.shape[1:])


def gy_moves(size):
    ring = size // 2
    swap = [(2 * k + c, 2 * k + 1 - c) for k in range(ring) for c in range(2)]
    turns = [[(2 * k + c, 2 * ((k + d) % ring) + c) for k in range(ring) for c in range(2)] for d in (1, 2, 3)]
    return swap, turns


def sum_gy_small(p, size):
    swap, turns = gy_moves(size)
    p = p + lax.ppermute(p, "gy", swap)
    got = [lax.ppermute(p, "gy", turn) for turn in turns]
    return (p + got[1]) + (got[0] + got[2])


def sum_gy(z, size, square=None):
    swap, turns = gy_moves(size)
    core = lax.axis_index("gy") % 2
    half = z.shape[0] // 2
    mine = lax.dynamic_slice_in_dim(z, core * half, half, 0)
    other = lax.dynamic_slice_in_dim(z, (1 - core) * half, half, 0)
    mine = mine + lax.ppermute(other, "gy", swap)
    inv = None
    if square is not None:
        mine, square = lax.optimization_barrier((mine, square))
    got = [lax.ppermute(mine, "gy", turn) for turn in turns]
    if square is not None:
        got, inv = lax.optimization_barrier((got, chol_inverse(square)))
    total = (mine + got[1]) + (got[0] + got[2])
    rest = lax.ppermute(total, "gy", swap)
    first = core == 0
    full = jnp.concatenate([jnp.where(first, total, rest), jnp.where(first, rest, total)], axis=0)
    return full, inv


def local(melt_field, start_time, start_x, *, gx, gy):
    cells_x, cells_y, time_len = melt_field.shape
    field = melt_field.reshape(cells_x * cells_y, time_len)
    gram = spread(sum_gy_small(scatter_sum(time_gram(field), "gx", gx), gy), "gx", gx)
    time_basis, shrunk, v = project(gram, start_time, start_x, melt_field)
    cols = shrunk.shape[1]
    v = spread(scatter_sum(v, "gx", gx), "gx", gx)
    z, _ = sum_gy(precise(v, shrunk, 1), gy)
    for sweep in range(SWEEPS_X - 1):
        vc = jnp.concatenate([precise(z, shrunk, 0), precise(z, z, 1)], axis=1)
        vc = spread(scatter_sum(vc, "gx", gx), "gx", gx)
        z, inv = sum_gy(precise(vc[:, :cols], shrunk, 1), gy, vc[:, cols:])
        z = precise(inv, z, 0)
    inv = chol_inverse(spread(scatter_sum(precise(z, z, 1), "gx", gx), "gx", gx))
    u = precise(inv, z, 0)
    core = scatter_sum(precise(u, shrunk, 0), "gx", gx)
    return (time_basis, u.T, core)


def solution(mesh):
    in_specs = (P("gx", "gy", None), P(), P("gx", None))
    out_specs = (P(), P("gx", None), P("gx", "gy"))
    body = functools.partial(local, gx=mesh.shape["gx"], gy=mesh.shape["gy"])
    return jax.shard_map(body, mesh=mesh, in_specs=in_specs, out_specs=out_specs, check_vma=False)
```

```python
import functools

import jax
import jax.numpy as jnp
from jax import lax
from jax.experimental import pallas as pl
from jax.experimental.pallas import tpu as pltpu
from jax.sharding import PartitionSpec as P

ITERS_T = 8
SWEEPS_X = 3
F32 = jnp.float32
BF16 = jnp.bfloat16
HI = lax.Precision.HIGHEST


def split3(x):
    h = x.astype(BF16)
    rest = x - h.astype(F32)
    m = rest.astype(BF16)
    l = (rest - m.astype(F32)).astype(BF16)
    return h, m, l


def split2(x):
    h = x.astype(BF16)
    return h, (x - h.astype(F32)).astype(BF16)


def dot(a, b, ca=1, cb=0):
    return lax.dot_general(a, b, (((ca,), (cb,)), ((), ())), preferred_element_type=F32)


def inverse_factor(gram):
    n = gram.shape[0]
    tiles = n // 8
    left = [gram[8 * t : 8 * t + 8] for t in range(tiles)]
    row_id = lax.broadcasted_iota(jnp.int32, (8, n), 0)
    col_id = lax.broadcasted_iota(jnp.int32, (8, n), 1)
    right = [jnp.where(col_id == row_id + 8 * t, 1.0, 0.0).astype(F32) for t in range(tiles)]
    bc = lambda x, m: jnp.broadcast_to(x[m : m + 1], (8, n))
    lane = lambda x, j: jnp.broadcast_to(x[:, j : j + 1], (8, n))
    out = []
    cols = {(t, j): lane(left[t], j) for j in range(8) for t in range(tiles)}
    for b in range(tiles):
        for j in range(8 * b + 8, min(8 * b + 16, n)):
            for t in range(b + 1, tiles):
                cols[t, j] = lane(left[t], j)
        rows_l, rows_r = left[b], right[b]
        steps = []
        pivots = jnp.ones((8, n), F32)
        for m in range(0, 8, 2):
            c = 8 * b + m
            a, d, e = bc(cols[b, c], m), bc(cols[b, c + 1], m + 1), bc(cols[b, c + 1], m)
            ra = 1.0 / a
            ratio = e * ra
            rd = a * (1.0 / (a * d - e * e))
            pivots = jnp.where(row_id == m, a, jnp.where(row_id == m + 1, d - e * ratio, pivots))
            f0 = {t: cols[t, c] * ra for t in range(b, tiles)}
            f1 = {t: (cols[t, c + 1] - f0[t] * e) * rd for t in range(b, tiles)}
            f0[b] = jnp.where(row_id > m, f0[b], 0.0)
            f1[b] = jnp.where(row_id > m + 1, f1[b], 0.0)
            for j in range(c + 2, min(8 * b + 16, n)):
                tj, mj = j // 8, j % 8
                v0 = bc(cols[b, j], m) if tj == b else bc(cols[tj, c], mj)
                v1 = bc(cols[b, j], m + 1) if tj == b else bc(cols[tj, c + 1], mj)
                v1 = v1 - ratio * v0
                for t in range(tj, tiles):
                    cols[t, j] = (cols[t, j] - f0[t] * v0) - f1[t] * v1
            l0, r0 = bc(rows_l, m), bc(rows_r, m)
            l1, r1 = bc(rows_l, m + 1) - ratio * l0, bc(rows_r, m + 1) - ratio * r0
            rows_l = (rows_l - f0[b] * l0) - f1[b] * l1
            rows_r = (rows_r - f0[b] * r0) - f1[b] * r1
            steps += [(f0, l0, r0), (f1, l1, r1)]
        for t in range(b + 1, tiles):
            for factor, row_l, row_r in steps:
                left[t] = left[t] - factor[t] * row_l
                right[t] = right[t] - factor[t] * row_r
        out.append(rows_r * lax.rsqrt(pivots))
    return jnp.concatenate(out, axis=0)


def dot6(a, b, ca=1, cb=0):
    n = a.shape[0]
    h, m, l = split3(a)
    x = dot(jnp.concatenate([h, m, l], axis=0), b[0], ca, cb)
    y = dot(jnp.concatenate([h, m], axis=0), b[1], ca, cb)
    z = dot(h, b[2], ca, cb)
    return x[:n] + ((x[n : 2 * n] + y[:n]) + ((x[2 * n :] + y[n:]) + z))

def gram6(z):
    h, m, l = split3(z)
    a = jnp.concatenate([h, h, m, m, h, l], axis=1)
    b = jnp.concatenate([h, m, h, m, l, h], axis=1)
    return dot(a, b, 1, 1)


BLK = 32


def chol_kernel(c_ref, out_ref, work):
    n = c_ref.shape[0]
    col_id = lax.broadcasted_iota(jnp.int32, (BLK, n), 1)
    row_id = lax.broadcasted_iota(jnp.int32, (BLK, n), 0)
    work[...] = c_ref[...]
    diag = work[0:BLK, 0:BLK]
    for k in range(n // BLK):
        lo, hi = k * BLK, (k + 1) * BLK
        if hi < n:
            right = split3(work[lo:hi, hi : hi + BLK])
            below = work[hi : hi + BLK, lo:hi]
            after = work[hi : hi + BLK, hi : hi + BLK]
        in_blk = (col_id >= lo) & (col_id < hi)
        row = split3(jnp.where(in_blk, jnp.where(col_id - lo == row_id, 1.0, 0.0), work[lo:hi, :]))
        inv = inverse_factor(diag)
        if hi < n:
            panel = dot6(below, split3(inv), 1, 1)
            diag = after - dot6(panel, split3(dot6(inv, right)))
        r = dot6(inv, row)
        out_ref[lo:hi, :] = jnp.where(col_id < hi, r, 0.0)
        if hi < n:
            h, m, l = split3(r)
            xt = jnp.concatenate([h, h, m, m, h, l], axis=0)
            w = jnp.concatenate([h, m, h, m, l, h], axis=0)
            base = hi // 128 * 128
            upd = dot(xt[:, base:], w, 0, 0)
            cid = lax.broadcasted_iota(jnp.int32, (n - hi, n), 1)
            old = jnp.where((cid >= lo) & (cid < hi), 0.0, work[hi:, :])
            work[hi:, :] = old - upd[hi - base :, :]


def chol_inverse(c):
    n = c.shape[0]
    return pl.pallas_call(
        chol_kernel,
        out_shape=jax.ShapeDtypeStruct((n, n), F32),
        in_specs=[pl.BlockSpec(memory_space=pltpu.VMEM)],
        out_specs=pl.BlockSpec(memory_space=pltpu.VMEM),
        scratch_shapes=[pltpu.VMEM((n, n), F32)],
        compiler_params=pltpu.CompilerParams(vmem_limit_bytes=16 << 20),
        cost_estimate=pl.CostEstimate(flops=1 << 30, bytes_accessed=1 << 20, transcendentals=0),
    )(c)


CHUNKS = (512, 1536, 2048, 2048, 2048)


def gram_kernel(m_hbm, out_ref, buf, sems):
    copies, starts, at = [], [], 0
    for i, rows in enumerate(CHUNKS):
        span = pl.ds(at, rows)
        copies.append(pltpu.make_async_copy(m_hbm.at[span], buf.at[span], sems.at[i]))
        starts.append(at)
        at += rows
    for copy in copies:
        copy.start()
    high = cross = low = None
    for copy, at, rows in zip(copies, starts, CHUNKS):
        copy.wait()
        h, l = split2(buf[at : at + rows, :])
        hh, hl, ll = dot(h, h, 0, 0), dot(h, l, 0, 0), dot(l, l, 0, 0)
        high, cross, low = (hh, hl, ll) if high is None else (high + hh, cross + hl, low + ll)
    out_ref[...] = high + (cross + cross.T + low)


def time_gram(field):
    n = field.shape[1]
    assert field.shape[0] == sum(CHUNKS)
    return pl.pallas_call(
        gram_kernel,
        out_shape=jax.ShapeDtypeStruct((n, n), F32),
        in_specs=[pl.BlockSpec(memory_space=pl.ANY)],
        out_specs=pl.BlockSpec(memory_space=pltpu.VMEM),
        scratch_shapes=[pltpu.VMEM(field.shape, F32), pltpu.SemaphoreType.DMA((len(CHUNKS),))],
        compiler_params=pltpu.CompilerParams(vmem_limit_bytes=56 << 20),
    )(field)


def time_steps(g_ref, s_ref, gs):
    gs[0], gs[1], gs[2] = split3(g_ref[...])

    def apply_g(z):
        return dot6(z, (gs[0], gs[1], gs[2]))

    def step(_, z):
        y = apply_g(z)
        return dot6(inverse_factor(gram6(z)), split3(y))

    z = lax.fori_loop(0, ITERS_T - 1, step, apply_g(s_ref[...].T))
    return dot6(inverse_factor(gram6(z)), split3(z)).T


def dot3(a, b, cb=0):
    h, l = split2(a)
    return dot(h, b[0], 1, cb) + (dot(h, b[1], 1, cb) + dot(l, b[0], 1, cb))


def project_kernel(g_ref, s_ref, u_hbm, m_hbm, q_ref, shrunk_ref, v_ref, gs, by_y, weights, u_vmem, sems, u_sem):
    cells_y = m_hbm.shape[1]
    lanes = 128
    u_copy = pltpu.make_async_copy(u_hbm, u_vmem, u_sem)
    u_copy.start()
    copies = [pltpu.make_async_copy(m_hbm.at[:, y, :], by_y.at[y], sems.at[y]) for y in range(cells_y)]
    for copy in copies:
        copy.start()
    q = time_steps(g_ref, s_ref, gs)
    q_ref[...] = q
    rank = q.shape[1]
    per = lanes // rank
    qh, ql = split2(q)
    qh, ql = qh.astype(F32), ql.astype(F32)
    for k in range(per):
        pad = lambda a: jnp.pad(a, ((0, 0), (k * rank, lanes - (k + 1) * rank)))
        weights[k] = jnp.concatenate([pad(qh), pad(ql)], axis=1).astype(BF16)
    for copy in copies:
        copy.wait()
    for group in range(cells_y // per):
        wide = thin = None
        for k in range(per):
            h, l = split2(by_y[group * per + k])
            a, b = dot(h, weights[k]), dot(l, weights[k, :, :lanes])
            wide, thin = (a, b) if k == 0 else (wide + a, thin + b)
        h, l = split2(wide[:, :lanes] + (wide[:, lanes:] + thin))
        span = slice(group * lanes, (group + 1) * lanes)
        shrunk_ref[0, :, span], shrunk_ref[1, :, span] = h, l
    u_copy.wait()
    v_ref[...] = dot3(u_vmem[...].T, shrunk_ref)


def project(gram, start_time, start_x, field):
    cells_x, cells_y, n = field.shape
    rank = start_time.shape[1]
    cols = cells_y * rank
    vmem = pl.BlockSpec(memory_space=pltpu.VMEM)
    return pl.pallas_call(
        project_kernel,
        out_shape=(
            jax.ShapeDtypeStruct((n, rank), F32),
            jax.ShapeDtypeStruct((2, cells_x, cols), BF16),
            jax.ShapeDtypeStruct((start_x.shape[1], cols), F32),
        ),
        in_specs=[vmem, vmem, pl.BlockSpec(memory_space=pl.ANY), pl.BlockSpec(memory_space=pl.ANY)],
        out_specs=(vmem, vmem, vmem),
        scratch_shapes=[
            pltpu.VMEM((3, n, n), BF16),
            pltpu.VMEM((cells_y, cells_x, n), F32),
            pltpu.VMEM((128 // rank, n, 256), BF16),
            pltpu.VMEM(start_x.shape, F32),
            pltpu.SemaphoreType.DMA((cells_y,)),
            pltpu.SemaphoreType.DMA,
        ],
        compiler_params=pltpu.CompilerParams(vmem_limit_bytes=56 << 20),
    )(gram, start_time, start_x, field)


VMEM = pl.BlockSpec(memory_space=pltpu.VMEM)
SMEM = pl.BlockSpec(memory_space=pltpu.SMEM)


def on_core(kernel, out_shape, args, specs):
    return pl.pallas_call(
        kernel,
        out_shape=out_shape,
        in_specs=specs,
        out_specs=jax.tree.map(lambda _: VMEM, out_shape),
        compiler_params=pltpu.CompilerParams(vmem_limit_bytes=24 << 20),
    )(*args)


def block(*shape):
    return jax.ShapeDtypeStruct(shape, F32)


def back_kernel(core_ref, v_ref, s_ref, mine_ref, other_ref):
    z = dot3(v_ref[:, : s_ref.shape[2]], s_ref, 1)
    half = z.shape[0] // 2
    first = core_ref[0] == 0
    mine_ref[...] = jnp.where(first, z[:half], z[half:])
    other_ref[...] = jnp.where(first, z[half:], z[:half])


def back(core, v, shrunk):
    half = block(v.shape[0] // 2, shrunk.shape[1])
    return on_core(back_kernel, (half, half), (core, v, shrunk), [SMEM, VMEM, VMEM])


def joined(core_ref, mine_ref, rest_ref):
    first = core_ref[0] == 0
    mine, rest = mine_ref[...], rest_ref[...]
    return jnp.concatenate([jnp.where(first, mine, rest), jnp.where(first, rest, mine)], axis=0)


def first_kernel(core_ref, mine_ref, rest_ref, s_ref, out_ref):
    z = joined(core_ref, mine_ref, rest_ref)
    cols = s_ref.shape[2]
    out_ref[:, :cols] = dot3(z, s_ref)
    out_ref[:, cols:] = gram6(z)


def next_kernel(core_ref, mine_ref, rest_ref, inv_ref, s_ref, out_ref):
    z = dot6(inv_ref[...], split3(joined(core_ref, mine_ref, rest_ref)))
    cols = s_ref.shape[2]
    out_ref[:, :cols] = dot3(z, s_ref)
    out_ref[:, cols:] = gram6(z)


def last_kernel(core_ref, mine_ref, rest_ref, inv_ref, z_ref, c_ref):
    z = dot6(inv_ref[...], split3(joined(core_ref, mine_ref, rest_ref)))
    z_ref[...] = z
    c_ref[...] = gram6(z)


def finish_kernel(inv_ref, z_ref, s_ref, u_ref, core_ref):
    u = dot6(inv_ref[...], split3(z_ref[...]))
    u_ref[...] = u.T
    core_ref[...] = dot3(u, s_ref)


def fan_kernel(got_ref, out_ref):
    total = got_ref[0]
    for k in range(1, got_ref.shape[0]):
        total = total + got_ref[k]
    for k in range(out_ref.shape[0]):
        out_ref[k] = total


def sum_all(v, axis, size):
    parts = v.reshape(size, v.shape[0] // size, v.shape[1])
    got = lax.all_to_all(parts, axis, 0, 0, tiled=True)
    copies = on_core(fan_kernel, block(*got.shape), (got,), [VMEM])
    return lax.all_to_all(copies, axis, 0, 0, tiled=True).reshape(v.shape)


def scatter_sum(v, axis, size):
    parts = v.reshape((size, v.shape[0] // size) + v.shape[1:])
    return jnp.sum(lax.all_to_all(parts, axis, 0, 0, tiled=True), axis=0)


def spread(p, axis, size):
    copies = jnp.broadcast_to(p[None], (size,) + p.shape)
    got = lax.all_to_all(copies, axis, 0, 0, tiled=True)
    return got.reshape((size * p.shape[0],) + p.shape[1:])


def gy_moves(size):
    ring = size // 2
    swap = [(2 * k + c, 2 * k + 1 - c) for k in range(ring) for c in range(2)]
    turns = [[(2 * k + c, 2 * ((k + d) % ring) + c) for k in range(ring) for c in range(2)] for d in (1, 2, 3)]
    return swap, turns


def sum_gy_small(p, size):
    swap, turns = gy_moves(size)
    p = p + lax.ppermute(p, "gy", swap)
    got = [lax.ppermute(p, "gy", turn) for turn in turns]
    return (p + got[1]) + (got[0] + got[2])


def sum_gy(mine, other, size, square=None):
    swap, turns = gy_moves(size)
    mine = mine + lax.ppermute(other, "gy", swap)
    inv = None
    if square is not None:
        mine, square = lax.optimization_barrier((mine, square))
    got = [lax.ppermute(mine, "gy", turn) for turn in turns]
    if square is not None:
        got, inv = lax.optimization_barrier((got, chol_inverse(square)))
    total = (mine + got[1]) + (got[0] + got[2])
    return total, lax.ppermute(total, "gy", swap), inv


def local(melt_field, start_time, start_x, *, gx, gy):
    cells_x, cells_y, time_len = melt_field.shape
    field = melt_field.reshape(cells_x * cells_y, time_len)
    gram = spread(sum_gy_small(scatter_sum(time_gram(field), "gx", gx), gy), "gx", gx)
    time_basis, shrunk, v = project(gram, start_time, start_x, melt_field)
    rank, cols = v.shape
    core = (lax.axis_index("gy") % 2).astype(jnp.int32).reshape(1)
    where = [SMEM, VMEM, VMEM]
    mine, rest, _ = sum_gy(*back(core, sum_all(v, "gx", gx), shrunk), gy)
    payload = block(rank, cols + rank)
    vc = on_core(first_kernel, payload, (core, mine, rest, shrunk), where + [VMEM])
    for sweep in range(SWEEPS_X - 1):
        vc = sum_all(vc, "gx", gx)
        mine, rest, inv = sum_gy(*back(core, vc, shrunk), gy, vc[:, cols:])
        if sweep < SWEEPS_X - 2:
            vc = on_core(next_kernel, payload, (core, mine, rest, inv, shrunk), where + [VMEM] * 2)
    square = block(rank, rank)
    z, c = on_core(last_kernel, (block(rank, cells_x), square), (core, mine, rest, inv), where + [VMEM])
    inv = chol_inverse(sum_all(c, "gx", gx))
    shapes = (block(cells_x, rank), block(rank, cols))
    u, part = on_core(finish_kernel, shapes, (inv, z, shrunk), [VMEM] * 3)
    return (time_basis, u, scatter_sum(part, "gx", gx))


def solution(mesh):
    in_specs = (P("gx", "gy", None), P(), P("gx", None))
    out_specs = (P(), P("gx", None), P("gx", "gy"))
    body = functools.partial(local, gx=mesh.shape["gx"], gy=mesh.shape["gy"])
    return jax.shard_map(body, mesh=mesh, in_specs=in_specs, out_specs=out_specs, check_vma=False)
```

```python
import functools

import jax
import jax.numpy as jnp
from jax import lax
from jax.experimental import pallas as pl
from jax.experimental.pallas import tpu as pltpu
from jax.sharding import PartitionSpec as P

ITERS_T = 8
SWEEPS_X = 3
F32 = jnp.float32
BF16 = jnp.bfloat16
HI = lax.Precision.HIGHEST


def split3(x):
    h = x.astype(BF16)
    rest = x - h.astype(F32)
    m = rest.astype(BF16)
    l = (rest - m.astype(F32)).astype(BF16)
    return h, m, l


def split2(x):
    h = x.astype(BF16)
    return h, (x - h.astype(F32)).astype(BF16)


def dot(a, b, ca=1, cb=0):
    return lax.dot_general(a, b, (((ca,), (cb,)), ((), ())), preferred_element_type=F32)


def inverse_factor(gram):
    n = gram.shape[0]
    tiles = n // 8
    left = [gram[8 * t : 8 * t + 8] for t in range(tiles)]
    row_id = lax.broadcasted_iota(jnp.int32, (8, n), 0)
    col_id = lax.broadcasted_iota(jnp.int32, (8, n), 1)
    right = [jnp.where(col_id == row_id + 8 * t, 1.0, 0.0).astype(F32) for t in range(tiles)]
    bc = lambda x, m: jnp.broadcast_to(x[m : m + 1], (8, n))
    lane = lambda x, j: jnp.broadcast_to(x[:, j : j + 1], (8, n))
    out = []
    cols = {(t, j): lane(left[t], j) for j in range(8) for t in range(tiles)}
    for b in range(tiles):
        for j in range(8 * b + 8, min(8 * b + 16, n)):
            for t in range(b + 1, tiles):
                cols[t, j] = lane(left[t], j)
        rows_l, rows_r = left[b], right[b]
        steps = []
        pivots = jnp.ones((8, n), F32)
        for m in range(0, 8, 2):
            c = 8 * b + m
            a, d, e = bc(cols[b, c], m), bc(cols[b, c + 1], m + 1), bc(cols[b, c + 1], m)
            ra = 1.0 / a
            ratio = e * ra
            rd = a * (1.0 / (a * d - e * e))
            pivots = jnp.where(row_id == m, a, jnp.where(row_id == m + 1, d - e * ratio, pivots))
            f0 = {t: cols[t, c] * ra for t in range(b, tiles)}
            f1 = {t: (cols[t, c + 1] - f0[t] * e) * rd for t in range(b, tiles)}
            f0[b] = jnp.where(row_id > m, f0[b], 0.0)
            f1[b] = jnp.where(row_id > m + 1, f1[b], 0.0)
            for j in range(c + 2, min(8 * b + 16, n)):
                tj, mj = j // 8, j % 8
                v0 = bc(cols[b, j], m) if tj == b else bc(cols[tj, c], mj)
                v1 = bc(cols[b, j], m + 1) if tj == b else bc(cols[tj, c + 1], mj)
                v1 = v1 - ratio * v0
                for t in range(tj, tiles):
                    cols[t, j] = (cols[t, j] - f0[t] * v0) - f1[t] * v1
            l0, r0 = bc(rows_l, m), bc(rows_r, m)
            l1, r1 = bc(rows_l, m + 1) - ratio * l0, bc(rows_r, m + 1) - ratio * r0
            rows_l = (rows_l - f0[b] * l0) - f1[b] * l1
            rows_r = (rows_r - f0[b] * r0) - f1[b] * r1
            steps += [(f0, l0, r0), (f1, l1, r1)]
        for t in range(b + 1, tiles):
            for factor, row_l, row_r in steps:
                left[t] = left[t] - factor[t] * row_l
                right[t] = right[t] - factor[t] * row_r
        out.append(rows_r * lax.rsqrt(pivots))
    return jnp.concatenate(out, axis=0)


def dot6(a, b, ca=1, cb=0):
    n = a.shape[0]
    h, m, l = split3(a)
    x = dot(jnp.concatenate([h, m, l], axis=0), b[0], ca, cb)
    y = dot(jnp.concatenate([h, m], axis=0), b[1], ca, cb)
    z = dot(h, b[2], ca, cb)
    return x[:n] + ((x[n : 2 * n] + y[:n]) + ((x[2 * n :] + y[n:]) + z))

def gram6(z, w):
    h, m, l = split3(z)
    a = jnp.concatenate([h, h, m, m, h, l], axis=1)
    h, m, l = split3(w)
    b = jnp.concatenate([h, m, h, m, l, h], axis=1)
    return dot(a, b, 1, 1)


BLK = 32


def chol_kernel(core_ref, mine_ref, rest_ref, out_ref, work):
    n = mine_ref.shape[0]
    half = n // 2
    first = core_ref[0] == 0
    mine, rest = mine_ref[...], rest_ref[...]
    work[:, :half] = jnp.where(first, mine, rest)
    work[:, half:] = jnp.where(first, rest, mine)
    col_id = lax.broadcasted_iota(jnp.int32, (BLK, n), 1)
    row_id = lax.broadcasted_iota(jnp.int32, (BLK, n), 0)
    diag = work[0:BLK, 0:BLK]
    for k in range(n // BLK):
        lo, hi = k * BLK, (k + 1) * BLK
        if hi < n:
            right = split3(work[lo:hi, hi : hi + BLK])
            below = work[hi : hi + BLK, lo:hi]
            after = work[hi : hi + BLK, hi : hi + BLK]
        in_blk = (col_id >= lo) & (col_id < hi)
        row = split3(jnp.where(in_blk, jnp.where(col_id - lo == row_id, 1.0, 0.0), work[lo:hi, :]))
        inv = inverse_factor(diag)
        if hi < n:
            panel = dot6(below, split3(inv), 1, 1)
            diag = after - dot6(panel, split3(dot6(inv, right)))
        r = dot6(inv, row)
        out_ref[lo:hi, :] = jnp.where(col_id < hi, r, 0.0)
        if hi < n:
            h, m, l = split3(r)
            xt = jnp.concatenate([h, h, m, m, h, l], axis=0)
            w = jnp.concatenate([h, m, h, m, l, h], axis=0)
            base = hi // 128 * 128
            upd = dot(xt[:, base:], w, 0, 0)
            cid = lax.broadcasted_iota(jnp.int32, (n - hi, n), 1)
            old = jnp.where((cid >= lo) & (cid < hi), 0.0, work[hi:, :])
            work[hi:, :] = old - upd[hi - base :, :]


def chol_inverse(core, mine, rest):
    n = mine.shape[0]
    vmem = pl.BlockSpec(memory_space=pltpu.VMEM)
    return pl.pallas_call(
        chol_kernel,
        out_shape=jax.ShapeDtypeStruct((n, n), F32),
        in_specs=[pl.BlockSpec(memory_space=pltpu.SMEM), vmem, vmem],
        out_specs=vmem,
        scratch_shapes=[pltpu.VMEM((n, n), F32)],
        compiler_params=pltpu.CompilerParams(vmem_limit_bytes=16 << 20),
        cost_estimate=pl.CostEstimate(flops=1 << 30, bytes_accessed=1 << 20, transcendentals=0),
    )(core, mine, rest)


CHUNKS = (512, 1536, 2048, 2048, 2048)


def gram_kernel(m_hbm, out_ref, buf, sems):
    copies, starts, at = [], [], 0
    for i, rows in enumerate(CHUNKS):
        span = pl.ds(at, rows)
        copies.append(pltpu.make_async_copy(m_hbm.at[span], buf.at[span], sems.at[i]))
        starts.append(at)
        at += rows
    for copy in copies:
        copy.start()
    high = cross = low = None
    for copy, at, rows in zip(copies, starts, CHUNKS):
        copy.wait()
        h, l = split2(buf[at : at + rows, :])
        hh, hl, ll = dot(h, h, 0, 0), dot(h, l, 0, 0), dot(l, l, 0, 0)
        high, cross, low = (hh, hl, ll) if high is None else (high + hh, cross + hl, low + ll)
    out_ref[...] = high + (cross + cross.T + low)


def time_gram(field):
    n = field.shape[1]
    assert field.shape[0] == sum(CHUNKS)
    return pl.pallas_call(
        gram_kernel,
        out_shape=jax.ShapeDtypeStruct((n, n), F32),
        in_specs=[pl.BlockSpec(memory_space=pl.ANY)],
        out_specs=pl.BlockSpec(memory_space=pltpu.VMEM),
        scratch_shapes=[pltpu.VMEM(field.shape, F32), pltpu.SemaphoreType.DMA((len(CHUNKS),))],
        compiler_params=pltpu.CompilerParams(vmem_limit_bytes=50 << 20),
    )(field)


def time_steps(g_ref, s_ref, gs):
    gs[0], gs[1], gs[2] = split3(g_ref[...])

    def apply_g(z):
        return dot6(z, (gs[0], gs[1], gs[2]))

    def step(_, z):
        y = apply_g(z)
        return dot6(inverse_factor(gram6(z, z)), split3(y))

    z = lax.fori_loop(0, ITERS_T - 1, step, apply_g(s_ref[...]))
    return dot6(inverse_factor(gram6(z, z)), split3(z))


def dot3(a, b, cb=0):
    h, l = split2(a)
    return dot(h, b[0], 1, cb) + (dot(h, b[1], 1, cb) + dot(l, b[0], 1, cb))


def project_kernel(g_ref, s_ref, u_hbm, m_hbm, q_ref, shrunk_ref, v_ref, gs, by_y, weights, u_vmem, sems, u_sem):
    cells_y = m_hbm.shape[1]
    lanes = 128
    u_copy = pltpu.make_async_copy(u_hbm, u_vmem, u_sem)
    u_copy.start()
    copies = [pltpu.make_async_copy(m_hbm.at[:, y, :], by_y.at[y], sems.at[y]) for y in range(cells_y)]
    for copy in copies:
        copy.start()
    q_ref[...] = time_steps(g_ref, s_ref, gs)
    q = q_ref[...].T
    rank = q.shape[1]
    per = lanes // rank
    qh, ql = split2(q)
    qh, ql = qh.astype(F32), ql.astype(F32)
    for k in range(per):
        pad = lambda a: jnp.pad(a, ((0, 0), (k * rank, lanes - (k + 1) * rank)))
        weights[k] = jnp.concatenate([pad(qh), pad(ql)], axis=1).astype(BF16)
    for copy in copies:
        copy.wait()
    for group in range(cells_y // per):
        wide = thin = None
        for k in range(per):
            h, l = split2(by_y[group * per + k])
            a, b = dot(h, weights[k]), dot(l, weights[k, :, :lanes])
            wide, thin = (a, b) if k == 0 else (wide + a, thin + b)
        h, l = split2(wide[:, :lanes] + (wide[:, lanes:] + thin))
        span = slice(group * lanes, (group + 1) * lanes)
        shrunk_ref[0, :, span], shrunk_ref[1, :, span] = h, l
    u_copy.wait()
    v_ref[...] = dot3(u_vmem[...].T, shrunk_ref)


def project(gram, start_time, start_x, field):
    cells_x, cells_y, n = field.shape
    rank = start_time.shape[0]
    cols = cells_y * rank
    vmem = pl.BlockSpec(memory_space=pltpu.VMEM)
    return pl.pallas_call(
        project_kernel,
        out_shape=(
            jax.ShapeDtypeStruct((rank, n), F32),
            jax.ShapeDtypeStruct((2, cells_x, cols), BF16),
            jax.ShapeDtypeStruct((start_x.shape[1], cols), F32),
        ),
        in_specs=[vmem, vmem, pl.BlockSpec(memory_space=pl.ANY), pl.BlockSpec(memory_space=pl.ANY)],
        out_specs=(vmem, vmem, vmem),
        scratch_shapes=[
            pltpu.VMEM((3, n, n), BF16),
            pltpu.VMEM((cells_y, cells_x, n), F32),
            pltpu.VMEM((128 // rank, n, 256), BF16),
            pltpu.VMEM(start_x.shape, F32),
            pltpu.SemaphoreType.DMA((cells_y,)),
            pltpu.SemaphoreType.DMA,
        ],
        compiler_params=pltpu.CompilerParams(vmem_limit_bytes=50 << 20),
    )(gram, start_time, start_x, field)


VMEM = pl.BlockSpec(memory_space=pltpu.VMEM)
SMEM = pl.BlockSpec(memory_space=pltpu.SMEM)


def on_core(kernel, out_shape, args, specs):
    return pl.pallas_call(
        kernel,
        out_shape=out_shape,
        in_specs=specs,
        out_specs=jax.tree.map(lambda _: VMEM, out_shape),
        compiler_params=pltpu.CompilerParams(vmem_limit_bytes=24 << 20),
    )(*args)


def block(*shape):
    return jax.ShapeDtypeStruct(shape, F32)


def back_kernel(core_ref, v_ref, s_ref, mine_ref, other_ref):
    z = dot3(v_ref[:, : s_ref.shape[2]], s_ref, 1)
    half = z.shape[0] // 2
    first = core_ref[0] == 0
    mine_ref[...] = jnp.where(first, z[:half], z[half:])
    other_ref[...] = jnp.where(first, z[half:], z[:half])


def back(core, v, shrunk):
    half = block(v.shape[0] // 2, shrunk.shape[1])
    return on_core(back_kernel, (half, half), (core, v, shrunk), [SMEM, VMEM, VMEM])


def joined(core_ref, mine_ref, rest_ref):
    first = core_ref[0] == 0
    mine, rest = mine_ref[...], rest_ref[...]
    return jnp.concatenate([jnp.where(first, mine, rest), jnp.where(first, rest, mine)], axis=0)


def first_kernel(core_ref, mine_ref, rest_ref, s_ref, out_ref):
    z = joined(core_ref, mine_ref, rest_ref)
    cols = s_ref.shape[2]
    out_ref[:, :cols] = dot3(z, s_ref)
    half = z.shape[0] // 2
    out_ref[:, cols:] = gram6(z, jnp.where(core_ref[0] == 0, z[:half], z[half:]))


def next_kernel(core_ref, mine_ref, rest_ref, inv_ref, s_ref, out_ref):
    z = dot6(inv_ref[...], split3(joined(core_ref, mine_ref, rest_ref)))
    cols = s_ref.shape[2]
    out_ref[:, :cols] = dot3(z, s_ref)
    half = z.shape[0] // 2
    out_ref[:, cols:] = gram6(z, jnp.where(core_ref[0] == 0, z[:half], z[half:]))


def last_kernel(core_ref, mine_ref, rest_ref, inv_ref, z_ref, c_ref):
    z = dot6(inv_ref[...], split3(joined(core_ref, mine_ref, rest_ref)))
    z_ref[...] = z
    c_ref[...] = gram6(z, z)


def finish_kernel(inv_ref, z_ref, s_ref, u_ref, core_ref):
    u = dot6(inv_ref[...], split3(z_ref[...]))
    u_ref[...] = u.T
    core_ref[...] = dot3(u, s_ref)


def fan_kernel(got_ref, out_ref):
    total = got_ref[0]
    for k in range(1, got_ref.shape[0]):
        total = total + got_ref[k]
    for k in range(out_ref.shape[0]):
        out_ref[k] = total


def sum_all(v, axis, size):
    parts = v.reshape(size, v.shape[0] // size, v.shape[1])
    got = lax.all_to_all(parts, axis, 0, 0, tiled=True)
    copies = on_core(fan_kernel, block(*got.shape), (got,), [VMEM])
    return lax.all_to_all(copies, axis, 0, 0, tiled=True).reshape(v.shape)


def scatter_sum(v, axis, size):
    parts = v.reshape((size, v.shape[0] // size) + v.shape[1:])
    return jnp.sum(lax.all_to_all(parts, axis, 0, 0, tiled=True), axis=0)


def spread(p, axis, size):
    copies = jnp.broadcast_to(p[None], (size,) + p.shape)
    got = lax.all_to_all(copies, axis, 0, 0, tiled=True)
    return got.reshape((size * p.shape[0],) + p.shape[1:])


def gy_moves(size):
    ring = size // 2
    swap = [(2 * k + c, 2 * k + 1 - c) for k in range(ring) for c in range(2)]
    turns = [[(2 * k + c, 2 * ((k + d) % ring) + c) for k in range(ring) for c in range(2)] for d in (1, 2, 3)]
    return swap, turns


def sum_gy_small(p, size):
    swap, turns = gy_moves(size)
    p = p + lax.ppermute(p, "gy", swap)
    got = [lax.ppermute(p, "gy", turn) for turn in turns]
    return (p + got[1]) + (got[0] + got[2])


def sum_gy(core, mine, other, size, square=None):
    swap, turns = gy_moves(size)
    inv = None
    if square is not None:
        rest = lax.ppermute(square, "gy", swap)
    mine = mine + lax.ppermute(other, "gy", swap)
    if square is not None:
        mine, square, rest = lax.optimization_barrier((mine, square, rest))
    got = [lax.ppermute(mine, "gy", turn) for turn in turns]
    if square is not None:
        got, inv = lax.optimization_barrier((got, chol_inverse(core, square, rest)))
    total = (mine + got[1]) + (got[0] + got[2])
    return total, lax.ppermute(total, "gy", swap), inv


def local(melt_field, start_time, start_x, *, gx, gy):
    cells_x, cells_y, time_len = melt_field.shape
    field = melt_field.reshape(cells_x * cells_y, time_len)
    gram = spread(sum_gy_small(scatter_sum(time_gram(field), "gx", gx), gy), "gx", gx)
    time_basis, shrunk, v = project(gram, start_time.T, start_x, melt_field)
    rank, cols = v.shape
    half = rank // 2
    core = (lax.axis_index("gy") % 2).astype(jnp.int32).reshape(1)
    where = [SMEM, VMEM, VMEM]
    mine, rest, _ = sum_gy(core, *back(core, sum_all(v, "gx", gx), shrunk), gy)
    payload = block(rank, cols + half)
    vc = on_core(first_kernel, payload, (core, mine, rest, shrunk), where + [VMEM])
    for sweep in range(SWEEPS_X - 1):
        vc = sum_all(vc, "gx", gx)
        mine, rest, inv = sum_gy(core, *back(core, vc, shrunk), gy, vc[:, cols:])
        if sweep < SWEEPS_X - 2:
            vc = on_core(next_kernel, payload, (core, mine, rest, inv, shrunk), where + [VMEM] * 2)
    square = block(rank, rank)
    z, c = on_core(last_kernel, (block(rank, cells_x), square), (core, mine, rest, inv), where + [VMEM])
    c = sum_all(c, "gx", gx)
    inv = chol_inverse(jnp.zeros_like(core), c[:, :half], c[:, half:])
    shapes = (block(cells_x, rank), block(rank, cols))
    u, part = on_core(finish_kernel, shapes, (inv, z, shrunk), [VMEM] * 3)
    return (time_basis.T, u, scatter_sum(part, "gx", gx))


def solution(mesh):
    in_specs = (P("gx", "gy", None), P(), P("gx", None))
    out_specs = (P(), P("gx", None), P("gx", "gy"))
    body = functools.partial(local, gx=mesh.shape["gx"], gy=mesh.shape["gy"])
    return jax.shard_map(body, mesh=mesh, in_specs=in_specs, out_specs=out_specs, check_vma=False)
```

```python
import functools

import jax
import jax.numpy as jnp
from jax import lax
from jax.experimental import pallas as pl
from jax.experimental.pallas import tpu as pltpu
from jax.sharding import PartitionSpec as P

ITERS_T = 8
SWEEPS_X = 3
F32 = jnp.float32
BF16 = jnp.bfloat16
HI = lax.Precision.HIGHEST


def split3(x):
    h = x.astype(BF16)
    rest = x - h.astype(F32)
    m = rest.astype(BF16)
    l = (rest - m.astype(F32)).astype(BF16)
    return h, m, l


def split2(x):
    h = x.astype(BF16)
    return h, (x - h.astype(F32)).astype(BF16)


def dot(a, b, ca=1, cb=0):
    return lax.dot_general(a, b, (((ca,), (cb,)), ((), ())), preferred_element_type=F32)


def inverse_factor(gram):
    n = gram.shape[0]
    tiles = n // 8
    left = [gram[8 * t : 8 * t + 8] for t in range(tiles)]
    row_id = lax.broadcasted_iota(jnp.int32, (8, n), 0)
    col_id = lax.broadcasted_iota(jnp.int32, (8, n), 1)
    right = [jnp.where(col_id == row_id + 8 * t, 1.0, 0.0).astype(F32) for t in range(tiles)]
    bc = lambda x, m: jnp.broadcast_to(x[m : m + 1], (8, n))
    lane = lambda x, j: jnp.broadcast_to(x[:, j : j + 1], (8, n))
    out = []
    cols = {(t, j): lane(left[t], j) for j in range(8) for t in range(tiles)}
    for b in range(tiles):
        for j in range(8 * b + 8, min(8 * b + 16, n)):
            for t in range(b + 1, tiles):
                cols[t, j] = lane(left[t], j)
        rows_l, rows_r = left[b], right[b]
        steps = []
        pivots = jnp.ones((8, n), F32)
        for m in range(0, 8, 2):
            c = 8 * b + m
            a, d, e = bc(cols[b, c], m), bc(cols[b, c + 1], m + 1), bc(cols[b, c + 1], m)
            ra = 1.0 / a
            ratio = e * ra
            d = d - e * ratio
            rd = 1.0 / d
            pivots = jnp.where(row_id == m, a, jnp.where(row_id == m + 1, d, pivots))
            f0 = {t: cols[t, c] * ra for t in range(b, tiles)}
            f1 = {t: (cols[t, c + 1] - f0[t] * e) * rd for t in range(b, tiles)}
            f0[b] = jnp.where(row_id > m, f0[b], 0.0)
            f1[b] = jnp.where(row_id > m + 1, f1[b], 0.0)
            for j in range(c + 2, min(8 * b + 16, n)):
                tj, mj = j // 8, j % 8
                v0 = bc(cols[b, j], m) if tj == b else bc(cols[tj, c], mj)
                v1 = bc(cols[b, j], m + 1) if tj == b else bc(cols[tj, c + 1], mj)
                v1 = v1 - ratio * v0
                for t in range(tj, tiles):
                    cols[t, j] = (cols[t, j] - f0[t] * v0) - f1[t] * v1
            l0, r0 = bc(rows_l, m), bc(rows_r, m)
            l1, r1 = bc(rows_l, m + 1) - ratio * l0, bc(rows_r, m + 1) - ratio * r0
            rows_l = (rows_l - f0[b] * l0) - f1[b] * l1
            rows_r = (rows_r - f0[b] * r0) - f1[b] * r1
            steps += [(f0, l0, r0), (f1, l1, r1)]
        for t in range(b + 1, tiles):
            for factor, row_l, row_r in steps:
                left[t] = left[t] - factor[t] * row_l
                right[t] = right[t] - factor[t] * row_r
        out.append(rows_r * lax.rsqrt(pivots))
    return jnp.concatenate(out, axis=0)


def dot6(a, b, ca=1, cb=0):
    n = a.shape[0]
    h, m, l = split3(a)
    x = dot(jnp.concatenate([h, m, l], axis=0), b[0], ca, cb)
    y = dot(jnp.concatenate([h, m], axis=0), b[1], ca, cb)
    z = dot(h, b[2], ca, cb)
    return x[:n] + ((x[n : 2 * n] + y[:n]) + ((x[2 * n :] + y[n:]) + z))

def gram6(z, w):
    h, m, l = split3(z)
    a = jnp.concatenate([h, h, m, m, h, l], axis=1)
    h, m, l = split3(w)
    b = jnp.concatenate([h, m, h, m, l, h], axis=1)
    return dot(a, b, 1, 1)


BLK = 32


def chol_kernel(c_ref, out_ref, work):
    n = c_ref.shape[0]
    work[...] = c_ref[...]
    col_id = lax.broadcasted_iota(jnp.int32, (BLK, n), 1)
    row_id = lax.broadcasted_iota(jnp.int32, (BLK, n), 0)
    diag = work[0:BLK, 0:BLK]
    for k in range(n // BLK):
        lo, hi = k * BLK, (k + 1) * BLK
        if hi < n:
            right = split3(work[lo:hi, hi : hi + BLK])
            below = work[hi : hi + BLK, lo:hi]
            after = work[hi : hi + BLK, hi : hi + BLK]
        in_blk = (col_id >= lo) & (col_id < hi)
        row = split3(jnp.where(in_blk, jnp.where(col_id - lo == row_id, 1.0, 0.0), work[lo:hi, :]))
        inv = inverse_factor(diag)
        if hi < n:
            panel = dot6(below, split3(inv), 1, 1)
            diag = after - dot6(panel, split3(dot6(inv, right)))
        r = dot6(inv, row)
        out_ref[lo:hi, :] = jnp.where(col_id < hi, r, 0.0)
        if hi < n:
            h, m, l = split3(r)
            xt = jnp.concatenate([h, h, m, m, h, l], axis=0)
            w = jnp.concatenate([h, m, h, m, l, h], axis=0)
            base = hi // 128 * 128
            upd = dot(xt[:, base:], w, 0, 0)
            cid = lax.broadcasted_iota(jnp.int32, (n - hi, n), 1)
            old = jnp.where((cid >= lo) & (cid < hi), 0.0, work[hi:, :])
            work[hi:, :] = old - upd[hi - base :, :]


def chol_inverse(c):
    n = c.shape[0]
    vmem = pl.BlockSpec(memory_space=pltpu.VMEM)
    return pl.pallas_call(
        chol_kernel,
        out_shape=jax.ShapeDtypeStruct((n, n), F32),
        in_specs=[vmem],
        out_specs=vmem,
        scratch_shapes=[pltpu.VMEM((n, n), F32)],
        compiler_params=pltpu.CompilerParams(vmem_limit_bytes=16 << 20),
        cost_estimate=pl.CostEstimate(flops=1 << 30, bytes_accessed=1 << 20, transcendentals=0),
    )(c)


CHUNKS = (512, 1536, 2048, 2048, 2048)


def gram_kernel(m_hbm, out_ref, buf, sems):
    copies, starts, at = [], [], 0
    for i, rows in enumerate(CHUNKS):
        span = pl.ds(at, rows)
        copies.append(pltpu.make_async_copy(m_hbm.at[span], buf.at[span], sems.at[i]))
        starts.append(at)
        at += rows
    for copy in copies:
        copy.start()
    high = cross = low = None
    for copy, at, rows in zip(copies, starts, CHUNKS):
        copy.wait()
        h, l = split2(buf[at : at + rows, :])
        hh, hl, ll = dot(h, h, 0, 0), dot(h, l, 0, 0), dot(l, l, 0, 0)
        high, cross, low = (hh, hl, ll) if high is None else (high + hh, cross + hl, low + ll)
    out_ref[...] = high + (cross + cross.T + low)


def time_gram(field):
    n = field.shape[1]
    assert field.shape[0] == sum(CHUNKS)
    return pl.pallas_call(
        gram_kernel,
        out_shape=jax.ShapeDtypeStruct((n, n), F32),
        in_specs=[pl.BlockSpec(memory_space=pl.ANY)],
        out_specs=pl.BlockSpec(memory_space=pltpu.VMEM),
        scratch_shapes=[pltpu.VMEM(field.shape, F32), pltpu.SemaphoreType.DMA((len(CHUNKS),))],
        compiler_params=pltpu.CompilerParams(vmem_limit_bytes=50 << 20),
    )(field)


def time_steps(g_ref, s_ref, gs):
    gs[0], gs[1], gs[2] = split3(g_ref[...])

    def apply_g(z):
        return dot6(z, (gs[0], gs[1], gs[2]))

    def step(_, z):
        y = apply_g(z)
        return dot6(inverse_factor(gram6(z, z)), split3(y))

    z = lax.fori_loop(0, ITERS_T - 1, step, apply_g(s_ref[...]))
    return dot6(inverse_factor(gram6(z, z)), split3(z))


def project_kernel(g_ref, s_ref, u_hbm, m_hbm, q_ref, shrunk_ref, v_ref, gs, by_y, weights, u_vmem, sems, u_sem):
    cells_y = m_hbm.shape[1]
    lanes = 128
    u_copy = pltpu.make_async_copy(u_hbm, u_vmem, u_sem)
    u_copy.start()
    copies = [pltpu.make_async_copy(m_hbm.at[:, y, :], by_y.at[y], sems.at[y]) for y in range(cells_y)]
    for copy in copies:
        copy.start()
    q_ref[...] = time_steps(g_ref, s_ref, gs)
    q = q_ref[...].T
    rank = q.shape[1]
    per = lanes // rank
    qh, ql = split2(q)
    qh, ql = qh.astype(F32), ql.astype(F32)
    for k in range(per):
        pad = lambda a: jnp.pad(a, ((0, 0), (k * rank, lanes - (k + 1) * rank)))
        weights[k] = jnp.concatenate([pad(qh), pad(ql)], axis=1).astype(BF16)
    for copy in copies:
        copy.wait()
    for group in range(cells_y // per):
        wide = thin = None
        for k in range(per):
            h, l = split2(by_y[group * per + k])
            a, b = dot(h, weights[k]), dot(l, weights[k, :, :lanes])
            wide, thin = (a, b) if k == 0 else (wide + a, thin + b)
        span = slice(group * lanes, (group + 1) * lanes)
        for k, value in enumerate(split3(wide[:, :lanes] + (wide[:, lanes:] + thin))):
            shrunk_ref[k, :, span] = value
    u_copy.wait()
    v_ref[...] = dot6(u_vmem[...].T, shrunk_ref)


def project(gram, start_time, start_x, field):
    cells_x, cells_y, n = field.shape
    rank = start_time.shape[0]
    cols = cells_y * rank
    vmem = pl.BlockSpec(memory_space=pltpu.VMEM)
    return pl.pallas_call(
        project_kernel,
        out_shape=(
            jax.ShapeDtypeStruct((rank, n), F32),
            jax.ShapeDtypeStruct((3, cells_x, cols), BF16),
            jax.ShapeDtypeStruct((start_x.shape[1], cols), F32),
        ),
        in_specs=[vmem, vmem, pl.BlockSpec(memory_space=pl.ANY), pl.BlockSpec(memory_space=pl.ANY)],
        out_specs=(vmem, vmem, vmem),
        scratch_shapes=[
            pltpu.VMEM((3, n, n), BF16),
            pltpu.VMEM((cells_y, cells_x, n), F32),
            pltpu.VMEM((128 // rank, n, 256), BF16),
            pltpu.VMEM(start_x.shape, F32),
            pltpu.SemaphoreType.DMA((cells_y,)),
            pltpu.SemaphoreType.DMA,
        ],
        compiler_params=pltpu.CompilerParams(vmem_limit_bytes=50 << 20),
    )(gram, start_time, start_x, field)


VMEM = pl.BlockSpec(memory_space=pltpu.VMEM)
SMEM = pl.BlockSpec(memory_space=pltpu.SMEM)


def on_core(kernel, out_shape, args, specs):
    return pl.pallas_call(
        kernel,
        out_shape=out_shape,
        in_specs=specs,
        out_specs=jax.tree.map(lambda _: VMEM, out_shape),
        compiler_params=pltpu.CompilerParams(vmem_limit_bytes=24 << 20),
    )(*args)


def block(*shape):
    return jax.ShapeDtypeStruct(shape, F32)


def back_kernel(core_ref, v_ref, s_ref, mine_ref, other_ref):
    z = dot6(v_ref[:, : s_ref.shape[2]], s_ref, 1, 1)
    half = z.shape[0] // 2
    first = core_ref[0] == 0
    mine_ref[...] = jnp.where(first, z[:half], z[half:])
    other_ref[...] = jnp.where(first, z[half:], z[:half])


def back(core, v, shrunk):
    half = block(v.shape[0] // 2, shrunk.shape[1])
    return on_core(back_kernel, (half, half), (core, v, shrunk), [SMEM, VMEM, VMEM])


def joined(core_ref, mine_ref, rest_ref):
    first = core_ref[0] == 0
    mine, rest = mine_ref[...], rest_ref[...]
    return jnp.concatenate([jnp.where(first, mine, rest), jnp.where(first, rest, mine)], axis=0)


def join_kernel(core_ref, mine_ref, rest_ref, z_ref, c_ref):
    z = joined(core_ref, mine_ref, rest_ref)
    z_ref[...] = z
    c_ref[...] = gram6(z, z)


def next_kernel(inv_ref, z_ref, s_ref, out_ref):
    out_ref[...] = dot6(dot6(inv_ref[...], split3(z_ref[...])), s_ref)


def finish_kernel(inv_ref, z_ref, s_ref, u_ref, core_ref):
    u = dot6(inv_ref[...], split3(z_ref[...]))
    u_ref[...] = u.T
    core_ref[...] = dot6(u, s_ref)


def fan_kernel(got_ref, out_ref):
    total = got_ref[0]
    for k in range(1, got_ref.shape[0]):
        total = total + got_ref[k]
    for k in range(out_ref.shape[0]):
        out_ref[k] = total


def sum_all(v, axis, size):
    parts = v.reshape(size, v.shape[0] // size, v.shape[1])
    got = lax.all_to_all(parts, axis, 0, 0, tiled=True)
    copies = on_core(fan_kernel, block(*got.shape), (got,), [VMEM])
    return lax.all_to_all(copies, axis, 0, 0, tiled=True).reshape(v.shape)


def scatter_sum(v, axis, size):
    parts = v.reshape((size, v.shape[0] // size) + v.shape[1:])
    return jnp.sum(lax.all_to_all(parts, axis, 0, 0, tiled=True), axis=0)


def spread(p, axis, size):
    copies = jnp.broadcast_to(p[None], (size,) + p.shape)
    got = lax.all_to_all(copies, axis, 0, 0, tiled=True)
    return got.reshape((size * p.shape[0],) + p.shape[1:])


def gy_moves(size):
    ring = size // 2
    swap = [(2 * k + c, 2 * k + 1 - c) for k in range(ring) for c in range(2)]
    turns = [[(2 * k + c, 2 * ((k + d) % ring) + c) for k in range(ring) for c in range(2)] for d in (1, 2, 3)]
    return swap, turns


def sum_gy_small(p, size):
    swap, turns = gy_moves(size)
    p = p + lax.ppermute(p, "gy", swap)
    got = [lax.ppermute(p, "gy", turn) for turn in turns]
    return (p + got[1]) + (got[0] + got[2])


def sum_gy(mine, other, size):
    swap, turns = gy_moves(size)
    mine = mine + lax.ppermute(other, "gy", swap)
    got = [lax.ppermute(mine, "gy", turn) for turn in turns]
    total = (mine + got[1]) + (got[0] + got[2])
    return total, lax.ppermute(total, "gy", swap)


def local(melt_field, start_time, start_x, *, gx, gy):
    cells_x, cells_y, time_len = melt_field.shape
    field = melt_field.reshape(cells_x * cells_y, time_len)
    gram = spread(sum_gy_small(scatter_sum(time_gram(field), "gx", gx), gy), "gx", gx)
    time_basis, shrunk, v = project(gram, start_time.T, start_x, melt_field)
    rank, cols = v.shape
    core = (lax.axis_index("gy") % 2).astype(jnp.int32).reshape(1)
    shapes = (block(rank, cells_x), block(rank, rank))
    for sweep in range(SWEEPS_X):
        mine, rest = sum_gy(*back(core, sum_all(v, "gx", gx), shrunk), gy)
        z, c = on_core(join_kernel, shapes, (core, mine, rest), [SMEM, VMEM, VMEM])
        inv = chol_inverse(sum_all(c, "gx", gx))
        if sweep < SWEEPS_X - 1:
            v = on_core(next_kernel, block(rank, cols), (inv, z, shrunk), [VMEM] * 3)
    shapes = (block(cells_x, rank), block(rank, cols))
    u, part = on_core(finish_kernel, shapes, (inv, z, shrunk), [VMEM] * 3)
    return (time_basis.T, u, scatter_sum(part, "gx", gx))


def solution(mesh):
    in_specs = (P("gx", "gy", None), P(), P("gx", None))
    out_specs = (P(), P("gx", None), P("gx", "gy"))
    body = functools.partial(local, gx=mesh.shape["gx"], gy=mesh.shape["gy"])
    return jax.shard_map(body, mesh=mesh, in_specs=in_specs, out_specs=out_specs, check_vma=False)
```

```python
import functools

import jax
import jax.numpy as jnp
from jax import lax
from jax.experimental import pallas as pl
from jax.experimental.pallas import tpu as pltpu
from jax.sharding import PartitionSpec as P

ITERS_T = 8
SWEEPS_X = 3
F32 = jnp.float32
BF16 = jnp.bfloat16
HI = lax.Precision.HIGHEST


def split3(x):
    h = x.astype(BF16)
    rest = x - h.astype(F32)
    m = rest.astype(BF16)
    l = (rest - m.astype(F32)).astype(BF16)
    return h, m, l


def split2(x):
    h = x.astype(BF16)
    return h, (x - h.astype(F32)).astype(BF16)


def dot(a, b, ca=1, cb=0):
    return lax.dot_general(a, b, (((ca,), (cb,)), ((), ())), preferred_element_type=F32)


def inverse_factor(gram):
    n = gram.shape[0]
    tiles = n // 8
    left = [gram[8 * t : 8 * t + 8] for t in range(tiles)]
    row_id = lax.broadcasted_iota(jnp.int32, (8, n), 0)
    col_id = lax.broadcasted_iota(jnp.int32, (8, n), 1)
    right = [jnp.where(col_id == row_id + 8 * t, 1.0, 0.0).astype(F32) for t in range(tiles)]
    bc = lambda x, m: jnp.broadcast_to(x[m : m + 1], (8, n))
    lane = lambda x, j: jnp.broadcast_to(x[:, j : j + 1], (8, n))
    out = []
    cols = {(t, j): lane(left[t], j) for j in range(8) for t in range(tiles)}
    for b in range(tiles):
        for j in range(8 * b + 8, min(8 * b + 16, n)):
            for t in range(b + 1, tiles):
                cols[t, j] = lane(left[t], j)
        rows_l, rows_r = left[b], right[b]
        steps = []
        pivots = jnp.ones((8, n), F32)
        for m in range(0, 8, 2):
            c = 8 * b + m
            a, d, e = bc(cols[b, c], m), bc(cols[b, c + 1], m + 1), bc(cols[b, c + 1], m)
            ra = 1.0 / a
            ratio = e * ra
            d = d - e * ratio
            rd = 1.0 / d
            pivots = jnp.where(row_id == m, a, jnp.where(row_id == m + 1, d, pivots))
            f0 = {t: cols[t, c] * ra for t in range(b, tiles)}
            f1 = {t: (cols[t, c + 1] - f0[t] * e) * rd for t in range(b, tiles)}
            f0[b] = jnp.where(row_id > m, f0[b], 0.0)
            f1[b] = jnp.where(row_id > m + 1, f1[b], 0.0)
            for j in range(c + 2, min(8 * b + 16, n)):
                tj, mj = j // 8, j % 8
                v0 = bc(cols[b, j], m) if tj == b else bc(cols[tj, c], mj)
                v1 = bc(cols[b, j], m + 1) if tj == b else bc(cols[tj, c + 1], mj)
                v1 = v1 - ratio * v0
                for t in range(tj, tiles):
                    cols[t, j] = (cols[t, j] - f0[t] * v0) - f1[t] * v1
            l0, r0 = bc(rows_l, m), bc(rows_r, m)
            l1, r1 = bc(rows_l, m + 1) - ratio * l0, bc(rows_r, m + 1) - ratio * r0
            rows_l = (rows_l - f0[b] * l0) - f1[b] * l1
            rows_r = (rows_r - f0[b] * r0) - f1[b] * r1
            steps += [(f0, l0, r0), (f1, l1, r1)]
        for t in range(b + 1, tiles):
            for factor, row_l, row_r in steps:
                left[t] = left[t] - factor[t] * row_l
                right[t] = right[t] - factor[t] * row_r
        out.append(rows_r * lax.rsqrt(pivots))
    return jnp.concatenate(out, axis=0)


def dot6(a, b, ca=1, cb=0):
    n = a.shape[0]
    h, m, l = split3(a)
    x = dot(jnp.concatenate([h, m, l], axis=0), b[0], ca, cb)
    y = dot(jnp.concatenate([h, m], axis=0), b[1], ca, cb)
    z = dot(h, b[2], ca, cb)
    return x[:n] + ((x[n : 2 * n] + y[:n]) + ((x[2 * n :] + y[n:]) + z))

def gram6(z, w):
    h, m, l = split3(z)
    a = jnp.concatenate([h, h, m, m, h, l], axis=1)
    h, m, l = split3(w)
    b = jnp.concatenate([h, m, h, m, l, h], axis=1)
    return dot(a, b, 1, 1)


BLK = 32


def chol_kernel(c_ref, out_ref, work):
    n = c_ref.shape[0]
    work[...] = c_ref[...]
    col_id = lax.broadcasted_iota(jnp.int32, (BLK, n), 1)
    row_id = lax.broadcasted_iota(jnp.int32, (BLK, n), 0)
    diag = work[0:BLK, 0:BLK]
    for k in range(n // BLK):
        lo, hi = k * BLK, (k + 1) * BLK
        if hi < n:
            right = split3(work[lo:hi, hi : hi + BLK])
            below = work[hi : hi + BLK, lo:hi]
            after = work[hi : hi + BLK, hi : hi + BLK]
        in_blk = (col_id >= lo) & (col_id < hi)
        row = split3(jnp.where(in_blk, jnp.where(col_id - lo == row_id, 1.0, 0.0), work[lo:hi, :]))
        inv = inverse_factor(diag)
        if hi < n:
            panel = dot6(below, split3(inv), 1, 1)
            diag = after - dot6(panel, split3(dot6(inv, right)))
        r = dot6(inv, row)
        out_ref[lo:hi, :] = jnp.where(col_id < hi, r, 0.0)
        if hi < n:
            h, m, l = split3(r)
            xt = jnp.concatenate([h, h, m, m, h, l], axis=0)
            w = jnp.concatenate([h, m, h, m, l, h], axis=0)
            base = hi // 128 * 128
            upd = dot(xt[:, base:], w, 0, 0)
            cid = lax.broadcasted_iota(jnp.int32, (n - hi, n), 1)
            old = jnp.where((cid >= lo) & (cid < hi), 0.0, work[hi:, :])
            work[hi:, :] = old - upd[hi - base :, :]


def chol_inverse(c):
    n = c.shape[0]
    vmem = pl.BlockSpec(memory_space=pltpu.VMEM)
    return pl.pallas_call(
        chol_kernel,
        out_shape=jax.ShapeDtypeStruct((n, n), F32),
        in_specs=[vmem],
        out_specs=vmem,
        scratch_shapes=[pltpu.VMEM((n, n), F32)],
        compiler_params=pltpu.CompilerParams(vmem_limit_bytes=16 << 20),
        cost_estimate=pl.CostEstimate(flops=1 << 30, bytes_accessed=1 << 20, transcendentals=0),
    )(c)


CHUNKS = (512, 1536, 2048, 2048, 2048)


def gram_kernel(m_hbm, out_ref, buf, sems):
    copies, starts, at = [], [], 0
    for i, rows in enumerate(CHUNKS):
        span = pl.ds(at, rows)
        copies.append(pltpu.make_async_copy(m_hbm.at[span], buf.at[span], sems.at[i]))
        starts.append(at)
        at += rows
    for copy in copies:
        copy.start()
    high = cross = low = None
    for copy, at, rows in zip(copies, starts, CHUNKS):
        copy.wait()
        h, l = split2(buf[at : at + rows, :])
        hh, hl, ll = dot(h, h, 0, 0), dot(h, l, 0, 0), dot(l, l, 0, 0)
        high, cross, low = (hh, hl, ll) if high is None else (high + hh, cross + hl, low + ll)
    out_ref[...] = high + (cross + cross.T + low)


def time_gram(field):
    n = field.shape[1]
    assert field.shape[0] == sum(CHUNKS)
    return pl.pallas_call(
        gram_kernel,
        out_shape=jax.ShapeDtypeStruct((n, n), F32),
        in_specs=[pl.BlockSpec(memory_space=pl.ANY)],
        out_specs=pl.BlockSpec(memory_space=pltpu.VMEM),
        scratch_shapes=[pltpu.VMEM(field.shape, F32), pltpu.SemaphoreType.DMA((len(CHUNKS),))],
        compiler_params=pltpu.CompilerParams(vmem_limit_bytes=50 << 20),
    )(field)


def time_steps(g_ref, s_ref, gs):
    gs[0], gs[1], gs[2] = split3(g_ref[...])

    def apply_g(z):
        return dot6(z, (gs[0], gs[1], gs[2]))

    def step(_, z):
        y = apply_g(z)
        return dot6(inverse_factor(gram6(z, z)), split3(y))

    z = lax.fori_loop(0, ITERS_T - 1, step, apply_g(s_ref[...]))
    return dot6(inverse_factor(gram6(z, z)), split3(z))


def project_kernel(g_ref, s_ref, u_hbm, m_hbm, q_ref, shrunk_ref, v_ref, gs, by_y, weights, u_vmem, sems, u_sem):
    cells_y = m_hbm.shape[1]
    lanes = 128
    u_copy = pltpu.make_async_copy(u_hbm, u_vmem, u_sem)
    u_copy.start()
    copies = [pltpu.make_async_copy(m_hbm.at[:, y, :], by_y.at[y], sems.at[y]) for y in range(cells_y)]
    for copy in copies:
        copy.start()
    q_ref[...] = time_steps(g_ref, s_ref, gs)
    q = q_ref[...].T
    rank = q.shape[1]
    per = lanes // rank
    qh, ql = split2(q)
    qh, ql = qh.astype(F32), ql.astype(F32)
    for k in range(per):
        pad = lambda a: jnp.pad(a, ((0, 0), (k * rank, lanes - (k + 1) * rank)))
        weights[k] = jnp.concatenate([pad(qh), pad(ql)], axis=1).astype(BF16)
    for copy in copies:
        copy.wait()
    for group in range(cells_y // per):
        wide = thin = None
        for k in range(per):
            h, l = split2(by_y[group * per + k])
            a, b = dot(h, weights[k]), dot(l, weights[k, :, :lanes])
            wide, thin = (a, b) if k == 0 else (wide + a, thin + b)
        span = slice(group * lanes, (group + 1) * lanes)
        for k, value in enumerate(split3(wide[:, :lanes] + (wide[:, lanes:] + thin))):
            shrunk_ref[k, :, span] = value
    u_copy.wait()
    v_ref[...] = dot6(u_vmem[...].T, shrunk_ref)


def project(gram, start_time, start_x, field):
    cells_x, cells_y, n = field.shape
    rank = start_time.shape[0]
    cols = cells_y * rank
    vmem = pl.BlockSpec(memory_space=pltpu.VMEM)
    return pl.pallas_call(
        project_kernel,
        out_shape=(
            jax.ShapeDtypeStruct((rank, n), F32),
            jax.ShapeDtypeStruct((3, cells_x, cols), BF16),
            jax.ShapeDtypeStruct((start_x.shape[1], cols), F32),
        ),
        in_specs=[vmem, vmem, pl.BlockSpec(memory_space=pl.ANY), pl.BlockSpec(memory_space=pl.ANY)],
        out_specs=(vmem, vmem, vmem),
        scratch_shapes=[
            pltpu.VMEM((3, n, n), BF16),
            pltpu.VMEM((cells_y, cells_x, n), F32),
            pltpu.VMEM((128 // rank, n, 256), BF16),
            pltpu.VMEM(start_x.shape, F32),
            pltpu.SemaphoreType.DMA((cells_y,)),
            pltpu.SemaphoreType.DMA,
        ],
        compiler_params=pltpu.CompilerParams(vmem_limit_bytes=50 << 20),
    )(gram, start_time, start_x, field)


VMEM = pl.BlockSpec(memory_space=pltpu.VMEM)
SMEM = pl.BlockSpec(memory_space=pltpu.SMEM)


def on_core(kernel, out_shape, args, specs):
    return pl.pallas_call(
        kernel,
        out_shape=out_shape,
        in_specs=specs,
        out_specs=jax.tree.map(lambda _: VMEM, out_shape),
        compiler_params=pltpu.CompilerParams(vmem_limit_bytes=24 << 20),
    )(*args)


def block(*shape):
    return jax.ShapeDtypeStruct(shape, F32)


def back_kernel(core_ref, v_ref, s_ref, mine_ref, other_ref):
    z = dot6(v_ref[:, : s_ref.shape[2]], s_ref, 1, 1)
    half = z.shape[0] // 2
    first = core_ref[0] == 0
    mine_ref[...] = jnp.where(first, z[:half], z[half:])
    other_ref[...] = jnp.where(first, z[half:], z[:half])


def back(core, v, shrunk):
    half = block(v.shape[0] // 2, shrunk.shape[1])
    return on_core(back_kernel, (half, half), (core, v, shrunk), [SMEM, VMEM, VMEM])


def joined(core_ref, mine_ref, rest_ref):
    first = core_ref[0] == 0
    mine, rest = mine_ref[...], rest_ref[...]
    return jnp.concatenate([jnp.where(first, mine, rest), jnp.where(first, rest, mine)], axis=0)


def join_kernel(core_ref, mine_ref, rest_ref, z_ref, c_ref):
    z = joined(core_ref, mine_ref, rest_ref)
    z_ref[...] = z
    c_ref[...] = gram6(z, z)


def next_kernel(inv_ref, z_ref, s_ref, out_ref):
    out_ref[...] = dot6(dot6(inv_ref[...], split3(z_ref[...])), s_ref)


def finish_kernel(inv_ref, z_ref, s_ref, u_ref, core_ref):
    u = dot6(inv_ref[...], split3(z_ref[...]))
    u_ref[...] = u.T
    core_ref[...] = dot6(u, s_ref)


def fan_kernel(got_ref, out_ref):
    total = got_ref[0]
    for k in range(1, got_ref.shape[0]):
        total = total + got_ref[k]
    for k in range(out_ref.shape[0]):
        out_ref[k] = total


def sum_all(v, axis, size):
    parts = v.reshape(size, v.shape[0] // size, v.shape[1])
    got = lax.all_to_all(parts, axis, 0, 0, tiled=True)
    copies = on_core(fan_kernel, block(*got.shape), (got,), [VMEM])
    return lax.all_to_all(copies, axis, 0, 0, tiled=True).reshape(v.shape)


def scatter_sum(v, axis, size):
    parts = v.reshape((size, v.shape[0] // size) + v.shape[1:])
    return jnp.sum(lax.all_to_all(parts, axis, 0, 0, tiled=True), axis=0)


def spread(p, axis, size):
    copies = jnp.broadcast_to(p[None], (size,) + p.shape)
    got = lax.all_to_all(copies, axis, 0, 0, tiled=True)
    return got.reshape((size * p.shape[0],) + p.shape[1:])


def gy_moves(size):
    ring = size // 2
    swap = [(2 * k + c, 2 * k + 1 - c) for k in range(ring) for c in range(2)]
    turns = [[(2 * k + c, 2 * ((k + d) % ring) + c) for k in range(ring) for c in range(2)] for d in (1, 2, 3)]
    return swap, turns


def sum_gy_small(p, size):
    swap, turns = gy_moves(size)
    p = p + lax.ppermute(p, "gy", swap)
    got = [lax.ppermute(p, "gy", turn) for turn in turns]
    return (p + got[1]) + (got[0] + got[2])


def sum_gy(mine, other, size):
    swap, turns = gy_moves(size)
    mine = mine + lax.ppermute(other, "gy", swap)
    got = [lax.ppermute(mine, "gy", turn) for turn in turns]
    total = (mine + got[1]) + (got[0] + got[2])
    return total, lax.ppermute(total, "gy", swap)


def local(melt_field, start_time, start_x, *, gx, gy):
    cells_x, cells_y, time_len = melt_field.shape
    field = melt_field.reshape(cells_x * cells_y, time_len)
    core = (lax.axis_index("gy") % 2).astype(jnp.int32).reshape(1)
    part, core = lax.optimization_barrier((time_gram(field), core))
    gram = spread(sum_gy_small(scatter_sum(part, "gx", gx), gy), "gx", gx)
    time_basis, shrunk, v = project(gram, start_time.T, start_x, melt_field)
    rank, cols = v.shape
    shapes = (block(rank, cells_x), block(rank, rank))
    for sweep in range(SWEEPS_X):
        mine, rest = sum_gy(*back(core, sum_all(v, "gx", gx), shrunk), gy)
        z, c = on_core(join_kernel, shapes, (core, mine, rest), [SMEM, VMEM, VMEM])
        inv = chol_inverse(sum_all(c, "gx", gx))
        if sweep < SWEEPS_X - 1:
            v = on_core(next_kernel, block(rank, cols), (inv, z, shrunk), [VMEM] * 3)
    shapes = (block(cells_x, rank), block(rank, cols))
    u, part = on_core(finish_kernel, shapes, (inv, z, shrunk), [VMEM] * 3)
    return (time_basis.T, u, scatter_sum(part, "gx", gx))


def solution(mesh):
    in_specs = (P("gx", "gy", None), P(), P("gx", None))
    out_specs = (P(), P("gx", None), P("gx", "gy"))
    body = functools.partial(local, gx=mesh.shape["gx"], gy=mesh.shape["gy"])
    return jax.shard_map(body, mesh=mesh, in_specs=in_specs, out_specs=out_specs, check_vma=False)
```
